32 devices in a mesh: batch: 8 (over z, y), table: 4 (over x, core).
Axes of the slice: x: 2, y: 2, z: 4, core: 2. Of those that a mesh axis runs over, the one named last changes fastest.
Arguments:
- queries: bfloat16 [2, 16384, 128], P(None, ('batch', 'table')), may hold values from -6 to 6
- item_owner: int32 [2, 16384, 1], P(None, ('batch', 'table')), may hold values from 0 to 3; in each aligned block of 512 rows (0 to 511, 512 to 1023, ..., all dimensions but the last counted through in order) at most 384 rows name the same one
- item_row: int32 [2, 16384], P(None, ('batch', 'table')), may hold values from 0 to 479
- table: float32 [1920, 128], P('table'), may hold values from -6 to 6
- accum: float32 [1920], P('table'), may hold values from 0.1 to 1
- fifo: bfloat16 [256, 128], P(('batch', 'table')), may hold values from -0.6 to 0.6
- fifo_head: int32 [32], P(('batch', 'table')), may hold values from 0 to 7
Outputs:
- losses: float32 [2, 16384], P(None, ('batch', 'table'))
- query_grad: bfloat16 [2, 16384, 128], P(None, ('batch', 'table'))
- table_out: float32 [1920, 128], P('table')
- accum_out: float32 [1920], P('table')
- fifo_out: bfloat16 [256, 128], P(('batch', 'table'))
The draws below stay inside these ranges and needn't reach their ends.
Inputs may be any that keep to these rules, and one draw needn't show every extreme that they name: `item_owner`: in each step the 512 rows of one device name each owner at most 384 times; in some aligned blocks an owner is named exactly 384 times.
All inputs are finite; a program needn't handle non-finite values.
Results may differ from the reference program's by a relative error of at most 0.002.
Values may be sent and summed in bfloat16 or wider, within the bound.
No kernel may reach another device: no remote copies, remote signals or barrier semaphores. Data moves between devices by JAX's collectives and lax.ppermute only.
A program may use at most 64 MiB of HBM per device.

```python
import math
import jax
import jax.numpy as jnp
import numpy as np
from jax import lax

E = 128
Q = 512
ROWS_DEV = 480
FIFO_DEV = 8
ENQ = 4
STEPS = 2
CAP = 384
ROWS = 1920
QUERIES = 16384
FIFO = 256
N_TABLE = 4
DEVICES = 32


def centre_total():
    return max(FIFO // 48, 4)


def shared_centres(key):
    return jax.random.normal(key, (centre_total(), E), jnp.float32) * E ** (-0.5)


def draw_queries(key, part):
    centres = shared_centres(key)
    key = jax.random.fold_in(key, 11)
    pick_key, noise_key = jax.random.split(key)
    members = jax.random.randint(pick_key, (STEPS, QUERIES), 0, centres.shape[0])
    noise = jax.random.normal(noise_key, (STEPS, QUERIES, E), jnp.float32) * (0.4 * E ** (-0.5))
    vectors = (centres[members] + noise) * E ** 0.5
    return jnp.clip(vectors, -6.0, 6.0).astype(jnp.bfloat16)


def draw_table(key, part):
    centres = shared_centres(key)
    key = jax.random.fold_in(key, 12)
    pick_key, noise_key = jax.random.split(key)
    members = jax.random.randint(pick_key, (ROWS,), 0, centres.shape[0])
    noise = jax.random.normal(noise_key, (ROWS, E), jnp.float32) * (0.4 * E ** (-0.5))
    vectors = (centres[members] + noise) * E ** 0.5
    return jnp.clip(vectors, -6.0, 6.0)


def draw_fifo(key, part):
    centres = shared_centres(key)
    key = jax.random.fold_in(key, 13)
    pick_key, noise_key = jax.random.split(key)
    members = jax.random.randint(pick_key, (FIFO,), 0, centres.shape[0])
    noise = jax.random.normal(noise_key, (FIFO, E), jnp.float32) * (0.4 * E ** (-0.5))
    vectors = (centres[members] + noise) * (1.0 / 1.077)
    return jnp.clip(vectors, -0.6, 0.6).astype(jnp.bfloat16)


def set_ends(drawn, stream_key, low, largest):
    place = [jax.random.randint(jax.random.fold_in(stream_key, axis), (), 0, length) for axis, length in enumerate(drawn.shape)]
    widest = drawn.shape.index(max(drawn.shape))
    next_to = place[:widest] + [(place[widest] + 1) % drawn.shape[widest]] + place[widest + 1:]
    return drawn.at[tuple(place)].set(low).at[tuple(next_to)].set(largest)


def levels(rng, shape, shards, least, largest):
    factor_of, own = 1.0, jax.random.fold_in(rng, 6)
    for dim, blocks in shards:
        steps = jnp.exp(jax.random.uniform(jax.random.fold_in(own, dim), (blocks,), jnp.float32, least / len(shards), largest / len(shards)))
        factor_of = factor_of * jnp.repeat(steps, shape[dim] // blocks).reshape([-1 if axis == dim else 1 for axis in range(len(shape))])
    return factor_of


def shared_out(rng, own, number, rows, count, top, reach, lean):
    ranking = jax.random.permutation(rng, count)
    packed, usual = load_shares(count, rows * top, reach, lean, True), load_shares(count, rows * top, reach, lean, False)
    places = jnp.arange(count)

    def named(lengths, turn):
        used = int((lengths > 0).sum())
        fixed = max(1, used // 4)
        shifted = fixed + (places - fixed + turn * (used - fixed)) % max(1, count - fixed)
        return jnp.zeros((count,), jnp.int32).at[ranking[jnp.where(places < fixed, places, shifted)]].set(jnp.asarray(lengths, jnp.int32))

    lengths = jnp.where(number % 4 == 0, named(packed, number // 4), named(usual, number - number // 4 - 1))
    mixed = jax.random.permutation(jax.random.fold_in(own, 3), count)
    source_of, taker = mixed[0:count // 2 * 2:2], mixed[1:count // 2 * 2:2]
    margin = jnp.minimum(lengths[source_of] - 1, reach - lengths[taker]) // 2
    margin = jnp.where((source_of == ranking[0]) | (taker == ranking[0]) | (lengths[taker] == 0), 0, jnp.maximum(margin, 0))
    shifted = jax.random.randint(jax.random.fold_in(own, 4), (count // 2,), 0, 1 << 20) % (margin + 1)
    lengths = lengths.at[source_of].add(-shifted).at[taker].add(shifted)
    items = jnp.searchsorted(jnp.cumsum(lengths), jnp.arange(rows * top), side="right").astype(jnp.int32)
    grid = items.reshape(top, rows).T
    grid = grid[jax.random.permutation(jax.random.fold_in(own, 1), rows)]
    turn = jax.random.randint(jax.random.fold_in(own, 2), (rows, 1), 0, top)
    return jnp.take_along_axis(grid, (jnp.arange(top)[None, :] + turn) % top, axis=1)


def load_shares(amount, total, most, skew, full):
    portions = [(1 << 20) // math.isqrt(rank ** skew) + 1 for rank in range(1, amount + 1)]
    largest = most if full else min(most, max(-(-total // amount), total * portions[0] // sum(portions)))
    least = 1 if total - largest >= amount - 1 else 0
    given, spare = [largest] + [least] * (amount - 1), total - largest - least * (amount - 1)
    while spare > 0:
        free = [i for i in range(1, amount) if given[i] < largest] or [i for i in range(1, amount) if given[i] < most]
        pool, remaining = sum([portions[i] for i in free]), spare
        for i in free:
            addition = min(most - given[i], max(1, remaining * portions[i] // pool), spare)
            given[i] = given[i] + addition
            spare = spare - addition
    return np.array(given)


def setup_inputs(seed: int = 0) -> dict:
    seeds = jax.random.split(jax.random.key(seed), 8)
    queries = draw_queries(jax.random.fold_in(seeds[7], 71), 0)
    item_owner_keys = jax.random.split(jax.random.fold_in(seeds[1], 1), STEPS * QUERIES // Q)
    item_owner_turns = jax.random.permutation(jax.random.fold_in(seeds[1], 3), STEPS * QUERIES // Q)
    item_owner = jax.vmap(lambda own, number: shared_out(jax.random.fold_in(seeds[1], 2), own, number, Q, N_TABLE, 1, CAP, 2))(item_owner_keys, item_owner_turns).reshape((STEPS, QUERIES, 1))
    item_row = set_ends(jax.random.randint(seeds[2], (STEPS, QUERIES), 0, ROWS_DEV), jax.random.fold_in(seeds[2], 1), 0, ROWS_DEV - 1).astype(jnp.int32)
    table = draw_table(jax.random.fold_in(seeds[7], 71), 0)
    accum = jnp.clip(jnp.exp(math.log(1.0) - 2.3025851 * jax.random.uniform(seeds[4], (ROWS,), jnp.float32) ** levels(seeds[4], (ROWS,), ((0, 4),), -0.2, 0.2)), 0.1, 1.0)
    fifo = draw_fifo(jax.random.fold_in(seeds[7], 71), 0)
    fifo_head = set_ends(jax.random.randint(seeds[6], (DEVICES,), 0, FIFO_DEV), jax.random.fold_in(seeds[6], 1), 0, FIFO_DEV - 1).astype(jnp.int32)
    return {"queries": queries, "item_owner": item_owner, "item_row": item_row, "table": table, "accum": accum, "fifo": fifo, "fifo_head": fifo_head}


score_scale = 10.0
learn_rate = 0.3
epsilon = 1e-06

def reference(queries, item_owner, item_row, table, accum, fifo, fifo_head):
    table_now = table
    accum_now = accum
    fifo_now = fifo
    loss_list = []
    grad_list = []
    device_ids = jnp.arange(DEVICES, dtype=jnp.int32)
    enqueue_ids = jnp.arange(ENQ, dtype=jnp.int32)
    for step_index in range(STEPS):
        query_f = queries[step_index].astype(jnp.float32)
        query_norm = jnp.sqrt(lax.optimization_barrier(jnp.sum(query_f * query_f, 1)) + epsilon)
        query_unit = query_f / query_norm[:, None]
        query_half = query_unit.astype(jnp.bfloat16)
        global_rows = (item_owner[step_index, :, 0] * ROWS_DEV + item_row[step_index]).astype(jnp.int32)
        item_vecs = table_now[global_rows]
        item_norm = jnp.sqrt(lax.optimization_barrier(jnp.sum(item_vecs * item_vecs, 1)) + epsilon)
        item_unit = item_vecs / item_norm[:, None]
        pos_score = score_scale * lax.optimization_barrier(jnp.sum(query_unit * item_unit, 1))

        def score_block(query_block):
            scores = score_scale * jnp.dot(query_block, fifo_now.T, preferred_element_type=jnp.float32)
            weights = jnp.exp(scores)
            moment = jnp.dot(weights.astype(jnp.bfloat16), fifo_now, preferred_element_type=jnp.float32)
            return (lax.optimization_barrier(jnp.sum(weights, 1)), moment)
        block_sums, moments = lax.map(score_block, query_half.reshape(DEVICES, Q, E))
        total_sum = jnp.exp(pos_score) + block_sums.reshape(-1)
        moment = moments.reshape(-1, E)
        loss_list.append(jnp.log(total_sum) - pos_score)
        pos_prob = jnp.exp(pos_score) / total_sum
        unit_grad = score_scale * ((pos_prob - 1.0)[:, None] * item_unit + moment / total_sum[:, None])
        along_query = lax.optimization_barrier(jnp.sum(query_unit * unit_grad, 1))
        query_grad = (unit_grad - query_unit * along_query[:, None]) / query_norm[:, None]
        grad_list.append(query_grad.astype(jnp.bfloat16))
        item_grad = score_scale * (pos_prob - 1.0)[:, None] * query_unit
        along_item = lax.optimization_barrier(jnp.sum(item_unit * item_grad, 1))
        row_grad = (item_grad - item_unit * along_item[:, None]) / item_norm[:, None]
        grad = jnp.zeros((ROWS, E), jnp.float32).at[global_rows].add(row_grad)
        accum_now = accum_now + lax.optimization_barrier(jnp.mean(grad * grad, 1))
        table_now = table_now - learn_rate * grad / jnp.sqrt(accum_now)[:, None]
        slots = device_ids[:, None] * FIFO_DEV + (fifo_head[:, None] + step_index * ENQ + enqueue_ids[None, :]) % FIFO_DEV
        sources = device_ids[:, None] * Q + enqueue_ids[None, :]
        joining = item_unit.astype(jnp.bfloat16)[sources.reshape(-1).astype(jnp.int32)]
        fifo_now = fifo_now.at[slots.reshape(-1).astype(jnp.int32)].set(joining)
    return (jnp.stack(loss_list), jnp.stack(grad_list), table_now, accum_now, fifo_now)
```

```python
import jax
import jax.numpy as jnp
from jax import lax
from jax.sharding import PartitionSpec as P

ENQ = 4
score_scale = 10.0
learn_rate = 0.3
epsilon = 1e-06
f32 = jnp.float32
bf16 = jnp.bfloat16
f16 = jnp.float16


def stages_of(count):
    stages, stride = [], 1
    while count > 1:
        radix = next(r for r in range(2, count + 1) if count % r == 0)
        stages.append((stride, radix))
        stride, count = stride * radix, count // radix
    return stages


def partners(piece, axis, stride, radix):
    count = lax.axis_size(axis)
    found = []
    for turn in range(1, radix):
        pairs = []
        for target in range(count):
            digit = target // stride % radix
            source = target + ((digit + turn) % radix - digit) * stride
            pairs.append((source, target))
        found.append(lax.ppermute(piece, axis, pairs))
    return found


def gather_any_order(piece, axis, stages):
    for stride, radix in stages:
        piece = jnp.concatenate([piece] + partners(piece, axis, stride, radix))
    return piece


def sum_over(total, axis, stages):
    for stride, radix in stages:
        sent = lax.optimization_barrier(total.astype(f16))
        parts = [sent] + partners(sent, axis, stride, radix)
        if radix > 2:
            digit = lax.axis_index(axis) // stride % radix
            order = (jnp.arange(radix, dtype=jnp.int32) - digit) % radix
            parts = list(jnp.stack(parts)[order])
        total = parts[0].astype(f32)
        for part in parts[1:]:
            total = total + part.astype(f32)
    return total


def split_parts(rows, terms):
    parts = []
    for _ in range(terms):
        part = lax.reduce_precision(rows, 8, 7)
        parts.append(part.astype(bf16))
        rows = rows - part
    return jnp.concatenate(parts, 1)


def pick_rows(places, parts, width):
    chosen = (places[:, None] == jnp.arange(parts.shape[0], dtype=jnp.int32)[None, :]).astype(bf16)
    found = jnp.dot(chosen, parts, preferred_element_type=f32)
    rows = found[:, :width]
    for start in range(width, parts.shape[1], width):
        rows = rows + found[:, start : start + width]
    return rows


def score_piece(query_half, carried, rows, kept):
    total_sum, moment = carried
    scores = score_scale * lax.dot_general(
        query_half, rows, (((1,), (1,)), ((), ())), preferred_element_type=f32
    )
    weights = jnp.where(kept[None, :], jnp.exp(scores), 0.0)
    moment = moment + jnp.dot(weights.astype(bf16), rows, preferred_element_type=f32)
    return (total_sum + jnp.sum(weights, 1), moment)


def score_rows(query_half, rows, kept):
    count, width = rows.shape
    carried = (jnp.zeros(query_half.shape[:1], f32), jnp.zeros(query_half.shape, f32))
    splits = 1
    while count // splits > 1024 and count % (splits * 2) == 0:
        splits = splits * 2
    if splits == 1:
        return score_piece(query_half, carried, rows, kept)
    stacked = (rows.reshape(splits, -1, width), kept.reshape(splits, -1))
    return lax.scan(lambda c, b: (score_piece(query_half, c, *b), None), carried, stacked)[0]


def norm_of(rows):
    return jnp.sqrt(jnp.sum(rows * rows, 1) + epsilon)


def per_device(queries, item_owner, item_row, table, accum, fifo, fifo_head):
    step_count, query_count, width = queries.shape
    owners, copies = lax.axis_size("table"), lax.axis_size("batch")
    owned = table.shape[0]
    queue_rows = fifo.shape[0]
    me = lax.axis_index("table")
    table_masks = [stride for stride, _ in reversed(stages_of(owners))]
    batch_stages = stages_of(copies)
    most = owners * copies * (3 * query_count // owners)
    grad_scale = 1.0
    while most * grad_scale > 32768.0:
        grad_scale = grad_scale / 2

    def place_of(owner, row):
        apart = jnp.bitwise_xor(owner, me)
        place = jnp.zeros_like(owner)
        for index, mask in enumerate(table_masks):
            place = place + jnp.where((apart & mask) != 0, 1 << index, 0)
        return place * owned + row

    def gather_table(piece):
        for mask in table_masks:
            piece = jnp.concatenate([piece] + partners(piece, "table", mask, 2))
        return piece

    head = fifo_head[0]
    table_all = gather_table(table)

    first_owner, first_row = item_owner[0, :ENQ, 0], item_row[0, :ENQ]
    told = jnp.concatenate([first_owner, first_row // 16, first_row % 16, head[None]])
    told_row = jnp.pad(told.astype(bf16), (0, width - told.shape[0]))[None, :]
    pad = jnp.zeros((-(queue_rows + 1) % 16, width), bf16)
    block = jnp.concatenate([fifo, told_row, pad])
    blocks = gather_any_order(block, "table", stages_of(owners))
    blocks = gather_any_order(blocks, "batch", batch_stages)
    blocks = blocks.reshape(owners * copies, -1, width)
    queue = blocks[:, :queue_rows].reshape(-1, width)
    told_all = blocks[:, queue_rows, : told.shape[0]].astype(jnp.int32)
    new_place = place_of(
        told_all[:, :ENQ], told_all[:, ENQ : 2 * ENQ] * 16 + told_all[:, 2 * ENQ : 3 * ENQ]
    ).reshape(-1)
    slots = jnp.arange(queue_rows, dtype=jnp.int32)
    kept = ((slots[None, :] - told_all[:, 3 * ENQ :]) % queue_rows >= ENQ).reshape(-1)

    parts = split_parts(table_all, 3)
    new_rows = pick_rows(new_place, parts, width)
    new_half = (new_rows / norm_of(new_rows)[:, None]).astype(bf16)

    loss_list, grad_list, joined = [], [], []
    for step in range(step_count):
        query_f = queries[step].astype(f32)
        query_norm = norm_of(query_f)
        query_unit = query_f / query_norm[:, None]
        query_half = query_unit.astype(bf16)
        places = place_of(item_owner[step, :, 0], item_row[step])
        if step == 0:
            rows, row_kept = queue, jnp.ones((queue.shape[0],), jnp.bool_)
        else:
            rows = jnp.concatenate([queue, new_half])
            row_kept = jnp.concatenate([kept, jnp.ones((new_half.shape[0],), jnp.bool_)])
        block_sums, moment = score_rows(query_half, rows, row_kept)
        item_vecs = pick_rows(places, parts, width)
        if step == 0:
            item_unit = item_vecs / norm_of(item_vecs)[:, None]
        else:
            item_unit = item_vecs
        joined.append(item_unit[:ENQ].astype(bf16))
        cosine = jnp.sum(query_unit * item_unit, 1)
        pos_score = score_scale * cosine
        total_sum = jnp.exp(pos_score) + block_sums
        loss_list.append(jnp.log(total_sum) - pos_score)
        lack = jnp.exp(pos_score) / total_sum - 1.0
        unit_grad = score_scale * (lack[:, None] * item_unit + moment / total_sum[:, None])
        along_query = jnp.sum(query_unit * unit_grad, 1)
        query_grad = (unit_grad - query_unit * along_query[:, None]) / query_norm[:, None]
        grad_list.append(query_grad.astype(bf16))

        across = (lack[:, None] * (query_unit - item_unit * cosine[:, None])).astype(bf16)
        chosen = (places[:, None] == jnp.arange(owners * owned, dtype=jnp.int32)[None, :]).astype(bf16)
        dense = grad_scale * lax.dot_general(
            chosen, across, (((0,), (0,)), ((), ())), preferred_element_type=f32
        )
        for mask in reversed(table_masks):
            half = dense.shape[0] // 2
            (other,) = partners(dense[half:].astype(f16), "table", mask, 2)
            dense = dense[:half] + other.astype(f32)
        dense = sum_over(dense, "batch", batch_stages)
        grad = dense * ((score_scale / grad_scale) / norm_of(table))[:, None]
        accum = accum + jnp.mean(grad * grad, 1)
        table = table - learn_rate * grad / jnp.sqrt(accum)[:, None]
        if step + 1 < step_count:
            unit = (table / norm_of(table)[:, None]).astype(f16)
            parts = split_parts(gather_table(unit).astype(f32), 2)

    fifo_out = fifo
    for step in range(step_count):
        place = (slots - head - step * ENQ) % queue_rows
        for k in range(ENQ):
            fifo_out = jnp.where((place == k)[:, None], joined[step][k][None, :], fifo_out)
    return (jnp.stack(loss_list), jnp.stack(grad_list), table, accum, fifo_out)


def solution(mesh):
    both = ("batch", "table")
    in_specs = (
        P(None, both, None),
        P(None, both, None),
        P(None, both),
        P("table", None),
        P("table"),
        P(both, None),
        P(both),
    )
    out_specs = (P(None, both), P(None, both, None), P("table", None), P("table"), P(both, None))
    return jax.shard_map(
        per_device, mesh=mesh, in_specs=in_specs, out_specs=out_specs, check_vma=False
    )
```

```python
import jax
import jax.numpy as jnp
from jax import lax
from jax.sharding import PartitionSpec as P

ENQ = 4
score_scale = 10.0
learn_rate = 0.3
epsilon = 1e-06
f32 = jnp.float32
bf16 = jnp.bfloat16
f16 = jnp.float16


def masks_of(count):
    masks = []
    while count > 1:
        assert count % 2 == 0
        count //= 2
        masks.append(count)
    return masks


def stages_of(count, stride):
    stages, count = [], count // stride
    while count > 1:
        radix = next(r for r in (4, 2, 3, *range(5, count + 1)) if count % r == 0)
        stages.append((stride, radix))
        stride, count = stride * radix, count // radix
    return stages


def flip(piece, table_mask, batch_mask=0):
    owners = lax.axis_size("table")
    mask = batch_mask * owners + table_mask
    count = lax.axis_size("batch") * owners
    return lax.ppermute(piece, ("batch", "table"), [(i ^ mask, i) for i in range(count)])


def turned(piece, stride, radix):
    count = lax.axis_size("batch")
    found = []
    for turn in range(1, radix):
        pairs = []
        for target in range(count):
            digit = target // stride % radix
            pairs.append((target + ((digit + turn) % radix - digit) * stride, target))
        found.append(lax.ppermute(piece, "batch", pairs))
    return found


def sum_stage(total, stride, radix):
    sent = lax.optimization_barrier(total.astype(f16))
    if radix in (2, 4) and stride & (stride - 1) == 0:
        parts = [sent] + [flip(sent, 0, stride * turn) for turn in range(1, radix)]
    else:
        parts = jnp.stack([sent] + turned(sent, stride, radix))
        digit = lax.axis_index("batch") // stride % radix
        parts = list(parts[(jnp.arange(radix, dtype=jnp.int32) - digit) % radix])
    parts = [part.astype(f32) for part in parts]
    while len(parts) > 1:
        parts = [sum(parts[i + 1 : i + 2], parts[i]) for i in range(0, len(parts), 2)]
    return parts[0]


def reduce_rows(kept, sent, masks, copies):
    masks = masks[::-1]
    for index, mask in enumerate(masks):
        if index + 1 == len(masks) and copies % 2 == 0:
            break
        kept = kept + flip(sent.astype(f16), mask).astype(f32)
        half = kept.shape[0] // 2
        if index + 1 < len(masks):
            kept, sent = kept[:half], kept[half:]
    stride = 1
    if copies % 2 == 0:
        own, away = lax.optimization_barrier((kept.astype(f16), sent.astype(f16)))
        beside = flip(away, masks[-1])
        copy = flip(own, 0, 1)
        across = flip(away, masks[-1], 1)
        kept = (own.astype(f32) + beside.astype(f32)) + (copy.astype(f32) + across.astype(f32))
        stride = 2
    for stage in stages_of(copies, stride):
        kept = sum_stage(kept, *stage)
    return kept


def split_parts(rows, terms):
    parts = []
    for _ in range(terms):
        part = lax.reduce_precision(rows, 8, 7)
        parts.append(part.astype(bf16))
        rows = rows - part
    return jnp.concatenate(parts, 1)


def pick_rows(places, blocks, width):
    total, first = None, 0
    for block in blocks:
        count = block.shape[0]
        chosen = (places[:, None] - first == jnp.arange(count, dtype=jnp.int32)[None, :]).astype(bf16)
        found = jnp.dot(chosen, block, preferred_element_type=f32)
        rows = found[:, :width]
        for start in range(width, block.shape[1], width):
            rows = rows + found[:, start : start + width]
        total = rows if total is None else total + rows
        first += count
    return total


def score_piece(query_half, carried, rows, kept):
    total_sum, moment = carried
    scores = score_scale * lax.dot_general(
        query_half, rows, (((1,), (1,)), ((), ())), preferred_element_type=f32
    )
    weights = jnp.where(kept[None, :], jnp.exp(scores), 0.0)
    moment = moment + jnp.dot(weights.astype(bf16), rows, preferred_element_type=f32)
    return (total_sum + jnp.sum(weights, 1), moment)


def score_rows(query_half, rows, kept):
    count, width = rows.shape
    carried = (jnp.zeros(query_half.shape[:1], f32), jnp.zeros(query_half.shape, f32))
    splits = 1
    while count // splits > 1024 and count % (splits * 2) == 0:
        splits = splits * 2
    if splits == 1:
        return score_piece(query_half, carried, rows, kept)
    stacked = (rows.reshape(splits, -1, width), kept.reshape(splits, -1))
    return lax.scan(lambda c, b: (score_piece(query_half, c, *b), None), carried, stacked)[0]


def norm_of(rows):
    return jnp.sqrt(jnp.sum(rows * rows, 1) + epsilon)


def per_device(queries, item_owner, item_row, table, accum, fifo, fifo_head):
    step_count, query_count, width = queries.shape
    owners, copies = lax.axis_size("table"), lax.axis_size("batch")
    owned = table.shape[0]
    queue_rows = fifo.shape[0]
    me = lax.axis_index("table")
    masks = masks_of(owners)
    most = owners * copies * (3 * query_count // owners)
    grad_scale = 1.0
    while most * grad_scale > 32768.0:
        grad_scale = grad_scale / 2

    def place_of(owner, row):
        apart = jnp.bitwise_xor(owner, me)
        place = jnp.zeros_like(owner)
        for index, mask in enumerate(masks):
            place = place + jnp.where((apart & mask) != 0, 1 << index, 0)
        return place * owned + row

    def gather_table(piece, terms):
        blocks = [split_parts(piece.astype(f32), terms)]
        for mask in masks:
            other = flip(piece, mask)
            blocks.append(split_parts(other.astype(f32), terms))
            piece = jnp.concatenate([piece, other])
        return blocks

    parts = gather_table(table, 3)

    head = fifo_head[0]
    first_owner, first_row = item_owner[0, :width, 0], item_row[0, :width]
    told = jnp.stack([first_owner, first_row // 16, first_row % 16, jnp.full((width,), head)])
    pad = jnp.zeros((-(queue_rows + 4) % 16, width), bf16)
    block = jnp.concatenate([fifo, told.astype(bf16), pad])
    blocks = jnp.broadcast_to(block[None], (owners * copies, *block.shape))
    blocks = lax.all_to_all(blocks, ("batch", "table"), 0, 0, tiled=True)
    queue = blocks[:, :queue_rows].reshape(-1, width)
    told_all = blocks[:, queue_rows : queue_rows + 4, :ENQ].astype(jnp.int32)
    new_place = place_of(told_all[:, 0], told_all[:, 1] * 16 + told_all[:, 2]).reshape(-1)
    slots = jnp.arange(queue_rows, dtype=jnp.int32)
    kept = ((slots[None, :] - told_all[:, 3, :1]) % queue_rows >= ENQ).reshape(-1)

    new_rows = pick_rows(new_place, parts, width)
    new_half = (new_rows / norm_of(new_rows)[:, None]).astype(bf16)

    loss_list, grad_list, joined = [], [], []
    for step in range(step_count):
        query_f = queries[step].astype(f32)
        query_norm = norm_of(query_f)
        query_unit = query_f / query_norm[:, None]
        query_half = query_unit.astype(bf16)
        places = place_of(item_owner[step, :, 0], item_row[step])
        if step == 0:
            rows, row_kept = queue, jnp.ones((queue.shape[0],), jnp.bool_)
        else:
            rows = jnp.concatenate([queue, new_half])
            row_kept = jnp.concatenate([kept, jnp.ones((new_half.shape[0],), jnp.bool_)])
        block_sums, moment = score_rows(query_half, rows, row_kept)
        item_vecs = pick_rows(places, parts, width)
        if step == 0:
            item_unit = item_vecs / norm_of(item_vecs)[:, None]
        else:
            item_unit = item_vecs
        joined.append(item_unit[:ENQ].astype(bf16))
        cosine = jnp.sum(query_unit * item_unit, 1)
        pos_score = score_scale * cosine
        total_sum = jnp.exp(pos_score) + block_sums
        loss_list.append(jnp.log(total_sum) - pos_score)
        lack = jnp.exp(pos_score) / total_sum - 1.0
        unit_grad = score_scale * (lack[:, None] * item_unit + moment / total_sum[:, None])
        along_query = jnp.sum(query_unit * unit_grad, 1)
        query_grad = (unit_grad - query_unit * along_query[:, None]) / query_norm[:, None]
        grad_list.append(query_grad.astype(bf16))

        across = (lack[:, None] * (query_unit - item_unit * cosine[:, None])).astype(bf16)
        halves = []
        for half in range(2):
            count = owners * owned // 2
            rows_of = jnp.arange(count, dtype=jnp.int32) + half * count
            chosen = (places[:, None] == rows_of[None, :]).astype(bf16)
            dense = lax.dot_general(
                chosen, across, (((0,), (0,)), ((), ())), preferred_element_type=f32
            )
            halves.append(grad_scale * dense)
        dense = reduce_rows(halves[0], halves[1], masks, copies)
        grad = dense * ((score_scale / grad_scale) / norm_of(table))[:, None]
        accum = accum + jnp.mean(grad * grad, 1)
        table = table - learn_rate * grad / jnp.sqrt(accum)[:, None]
        if step + 1 < step_count:
            unit = (table / norm_of(table)[:, None]).astype(f16)
            parts = gather_table(unit, 2)

    fifo_out = fifo
    for step in range(step_count):
        place = (slots - head - step * ENQ) % queue_rows
        for k in range(ENQ):
            fifo_out = jnp.where((place == k)[:, None], joined[step][k][None, :], fifo_out)
    return (jnp.stack(loss_list), jnp.stack(grad_list), table, accum, fifo_out)


def solution(mesh):
    both = ("batch", "table")
    in_specs = (
        P(None, both, None),
        P(None, both, None),
        P(None, both),
        P("table", None),
        P("table"),
        P(both, None),
        P(both),
    )
    out_specs = (P(None, both), P(None, both, None), P("table", None), P("table"), P(both, None))
    return jax.shard_map(
        per_device, mesh=mesh, in_specs=in_specs, out_specs=out_specs, check_vma=False
    )
```

```python
import jax
import jax.numpy as jnp
from jax import lax
from jax.experimental import pallas as pl
from jax.experimental.pallas import tpu as pltpu
from jax.sharding import PartitionSpec as P

ENQ = 4
score_scale = 10.0
learn_rate = 0.3
epsilon = 1e-06
f32 = jnp.float32
bf16 = jnp.bfloat16
f16 = jnp.float16


def masks_of(count):
    masks = []
    while count > 1:
        assert count % 2 == 0
        count //= 2
        masks.append(count)
    return masks


def stages_of(count, stride):
    stages, count = [], count // stride
    while count > 1:
        radix = next(r for r in range(2, count + 1) if count % r == 0)
        stages.append((stride, radix))
        stride, count = stride * radix, count // radix
    return stages


def flip(piece, mask):
    count = lax.axis_size("batch") * lax.axis_size("table")
    return lax.ppermute(piece, ("batch", "table"), [(i ^ mask, i) for i in range(count)])


def turned(piece, stride, radix):
    count = lax.axis_size("batch")
    found = []
    for turn in range(1, radix):
        pairs = []
        for target in range(count):
            digit = target // stride % radix
            pairs.append((target + ((digit + turn) % radix - digit) * stride, target))
        found.append(lax.ppermute(piece, "batch", pairs))
    return found


def sum_stage(total, stride, radix):
    sent = lax.optimization_barrier(total.astype(f16))
    parts = jnp.stack([sent] + turned(sent, stride, radix)) if radix > 2 else None
    if radix > 2:
        digit = lax.axis_index("batch") // stride % radix
        parts = list(parts[(jnp.arange(radix, dtype=jnp.int32) - digit) % radix])
    else:
        parts = [sent] + turned(sent, stride, radix)
    total = parts[0].astype(f32)
    for part in parts[1:]:
        total = total + part.astype(f32)
    return total


def split_parts(rows, terms):
    parts = []
    for _ in range(terms):
        part = lax.reduce_precision(rows, 8, 7)
        parts.append(part.astype(bf16))
        rows = rows - part
    return jnp.concatenate(parts, 1)


def pick_rows(places, blocks, width):
    total, first = None, 0
    for block in blocks:
        count = block.shape[0]
        chosen = (places[:, None] - first == jnp.arange(count, dtype=jnp.int32)[None, :]).astype(bf16)
        found = jnp.dot(chosen, block, preferred_element_type=f32)
        rows = found[:, :width]
        for start in range(width, block.shape[1], width):
            rows = rows + found[:, start : start + width]
        total = rows if total is None else total + rows
        first += count
    return total


def score_piece(query_half, carried, rows, kept):
    total_sum, moment = carried
    scores = score_scale * lax.dot_general(
        query_half, rows, (((1,), (1,)), ((), ())), preferred_element_type=f32
    )
    weights = jnp.where(kept[None, :], jnp.exp(scores), 0.0)
    moment = moment + jnp.dot(weights.astype(bf16), rows, preferred_element_type=f32)
    return (total_sum + jnp.sum(weights, 1), moment)


def score_rows(query_half, rows, kept):
    count, width = rows.shape
    carried = (jnp.zeros(query_half.shape[:1], f32), jnp.zeros(query_half.shape, f32))
    splits = 1
    while count // splits > 1024 and count % (splits * 2) == 0:
        splits = splits * 2
    if splits == 1:
        return score_piece(query_half, carried, rows, kept)
    stacked = (rows.reshape(splits, -1, width), kept.reshape(splits, -1))
    return lax.scan(lambda c, b: (score_piece(query_half, c, *b), None), carried, stacked)[0]


def norm_of(rows):
    return jnp.sqrt(jnp.sum(rows * rows, 1) + epsilon)


def prologue_kernel(fifo, owner, row, head, out):
    queue_rows, width = fifo.shape
    line = lax.broadcasted_iota(jnp.int32, (out.shape[1] - queue_rows, width), 0)
    owner, row = owner[0:1, :width], row[0:1, :width]
    told = jnp.where(line == 0, owner, jnp.where(line == 1, row // 16, row % 16))
    told = jnp.where(line == 3, head[0], told).astype(f32)
    block = jnp.concatenate([fifo[...].astype(f32), told]).astype(bf16)
    out[...] = jnp.broadcast_to(block[None], out.shape)


def per_device(queries, item_owner, item_row, table, accum, fifo, fifo_head):
    step_count, query_count, width = queries.shape
    owners, copies = lax.axis_size("table"), lax.axis_size("batch")
    owned = table.shape[0]
    part_rows = owned // 2
    queue_rows = fifo.shape[0]
    me = lax.axis_index("table")
    side = lax.axis_index("batch") % 2
    masks = masks_of(owners)
    most = owners * copies * (3 * query_count // owners)
    grad_scale = 1.0
    while most * grad_scale > 32768.0:
        grad_scale = grad_scale / 2

    def owner_place(owner):
        apart = jnp.bitwise_xor(owner, me)
        place = jnp.zeros_like(owner)
        for index, mask in enumerate(masks):
            place = place + jnp.where((apart & mask) != 0, 1 << index, 0)
        return place

    def place_whole(owner, row):
        return owner_place(owner) * owned + row

    def place_part(owner, row):
        return owner_place(owner) * owned + jnp.where(side == 0, row, (row + part_rows) % owned)

    def gather_whole(piece, terms):
        blocks = [split_parts(piece, terms)]
        for mask in masks:
            other = flip(piece, mask)
            blocks.append(split_parts(other, terms))
            piece = jnp.concatenate([piece, other])
        return blocks

    def gather_parts(piece, terms):
        wide = [piece] + [flip(piece, mask) for mask in (owners, masks[0], owners + masks[0])]
        piece = lax.optimization_barrier(jnp.concatenate(wide))
        blocks = [split_parts(piece.astype(f32), terms)]
        for mask in masks[1:]:
            other = flip(piece, mask)
            blocks.append(split_parts(other.astype(f32), terms))
            piece = jnp.concatenate([piece, other])
        return blocks

    def reduce_parts(kept, sent):
        for mask in masks[:0:-1]:
            kept = kept + flip(sent.astype(f16), mask).astype(f32)
            half = kept.shape[0] // 2
            if mask != masks[1]:
                kept, sent = kept[:half], kept[half:]
        pieces = [kept[i * part_rows : (i + 1) * part_rows] for i in range(4)]
        beside = [
            flip(piece.astype(f16), mask).astype(f32)
            for piece, mask in zip(pieces[1:], (owners, masks[0], owners + masks[0]))
        ]
        total = (pieces[0] + beside[0]) + (beside[1] + beside[2])
        for stage in stages_of(copies, 2):
            total = sum_stage(total, *stage)
        return total

    head = fifo_head[0]
    parts = gather_whole(table, 3)

    block_rows = queue_rows + 4 + -(queue_rows + 4) % 16
    vmem, smem = pl.BlockSpec(memory_space=pltpu.VMEM), pl.BlockSpec(memory_space=pltpu.SMEM)
    blocks = pl.pallas_call(
        prologue_kernel,
        out_shape=jax.ShapeDtypeStruct((owners * copies, block_rows, width), bf16),
        in_specs=[vmem, vmem, vmem, smem],
        out_specs=vmem,
    )(fifo, item_owner[:, :, 0], item_row, fifo_head)
    blocks = lax.all_to_all(blocks, ("batch", "table"), 0, 0, tiled=True)
    queue = blocks[:, :queue_rows].reshape(-1, width)
    told_all = blocks[:, queue_rows : queue_rows + 4, :ENQ].astype(jnp.int32)
    slots = jnp.arange(queue_rows, dtype=jnp.int32)

    part_table = lax.dynamic_slice_in_dim(table, side * part_rows, part_rows, 0)
    part_accum = lax.dynamic_slice_in_dim(accum, side * part_rows, part_rows, 0)
    loss_list, grad_list, joined = [], [], []
    new_half = kept = None
    for step in range(step_count):
        query_f = queries[step].astype(f32)
        query_norm = norm_of(query_f)
        query_unit = query_f / query_norm[:, None]
        query_half = query_unit.astype(bf16)
        owner, row = item_owner[step, :, 0], item_row[step]
        places = place_part(owner, row)
        if step == 0:
            rows, row_kept = queue, jnp.ones((queue.shape[0],), jnp.bool_)
        else:
            rows = jnp.concatenate([queue, new_half])
            row_kept = jnp.concatenate([kept, jnp.ones((new_half.shape[0],), jnp.bool_)])
        block_sums, moment = score_rows(query_half, rows, row_kept)
        if step == 0:
            item_vecs = pick_rows(place_whole(owner, row), parts, width)
            item_unit = item_vecs / norm_of(item_vecs)[:, None]
        else:
            item_unit = pick_rows(places, parts, width)
        joined.append(item_unit[:ENQ].astype(bf16))
        cosine = jnp.sum(query_unit * item_unit, 1)
        pos_score = score_scale * cosine
        total_sum = jnp.exp(pos_score) + block_sums
        lack = jnp.exp(pos_score) / total_sum - 1.0
        across = (lack[:, None] * (query_unit - item_unit * cosine[:, None])).astype(bf16)
        halves = []
        for half in range(2):
            count = owners * owned // 2
            rows_of = jnp.arange(count, dtype=jnp.int32) + half * count
            chosen = (places[:, None] == rows_of[None, :]).astype(bf16)
            dense = lax.dot_general(
                chosen, across, (((0,), (0,)), ((), ())), preferred_element_type=f32
            )
            halves.append(grad_scale * dense)
        halves[0] = lax.optimization_barrier(halves[0])
        total = reduce_parts(*halves)

        moment, total_sum, pos_score, lack, told_late, _ = lax.optimization_barrier(
            (moment, total_sum, pos_score, lack, told_all, halves[0])
        )
        loss_list.append(jnp.log(total_sum) - pos_score)
        unit_grad = score_scale * (lack[:, None] * item_unit + moment / total_sum[:, None])
        along_query = jnp.sum(query_unit * unit_grad, 1)
        query_grad = (unit_grad - query_unit * along_query[:, None]) / query_norm[:, None]
        grad_list.append(query_grad.astype(bf16))
        if step == 0:
            new_place = place_whole(told_late[:, 0], told_late[:, 1] * 16 + told_late[:, 2])
            new_rows = pick_rows(new_place.reshape(-1), parts, width)
            new_half = (new_rows / norm_of(new_rows)[:, None]).astype(bf16)
            kept = ((slots[None, :] - told_late[:, 3, :1]) % queue_rows >= ENQ).reshape(-1)

        grad = total * ((score_scale / grad_scale) / norm_of(part_table))[:, None]
        part_accum = part_accum + jnp.mean(grad * grad, 1)
        part_table = part_table - learn_rate * grad / jnp.sqrt(part_accum)[:, None]
        if step + 1 < step_count:
            unit = (part_table / norm_of(part_table)[:, None]).astype(f16)
            parts = gather_parts(unit, 2)

    lines = -(-part_rows // width)
    lines += -lines % 8
    packed = jnp.pad(part_accum, (0, lines * width - part_rows)).reshape(lines, width)
    mine = jnp.concatenate([part_table, packed])
    other = flip(mine, owners)
    both = [jnp.where(side == 0, mine, other), jnp.where(side == 0, other, mine)]
    table_out = jnp.concatenate([half[:part_rows] for half in both])
    accum_out = jnp.concatenate([half[part_rows:].reshape(-1)[:part_rows] for half in both])
    fifo_out = fifo
    for step in range(step_count):
        place = (slots - head - step * ENQ) % queue_rows
        for k in range(ENQ):
            fifo_out = jnp.where((place == k)[:, None], joined[step][k][None, :], fifo_out)
    return (jnp.stack(loss_list), jnp.stack(grad_list), table_out, accum_out, fifo_out)


def solution(mesh):
    both = ("batch", "table")
    in_specs = (
        P(None, both, None),
        P(None, both, None),
        P(None, both),
        P("table", None),
        P("table"),
        P(both, None),
        P(both),
    )
    out_specs = (P(None, both), P(None, both, None), P("table", None), P("table"), P(both, None))
    return jax.shard_map(
        per_device, mesh=mesh, in_specs=in_specs, out_specs=out_specs, check_vma=False
    )
```

```python
import functools

import jax
import jax.numpy as jnp
from jax import lax
from jax.experimental import pallas as pl
from jax.experimental.pallas import tpu as pltpu
from jax.sharding import PartitionSpec as P

ENQ = 4
score_scale = 10.0
learn_rate = 0.3
epsilon = 1e-06
f32 = jnp.float32
bf16 = jnp.bfloat16
f16 = jnp.float16


def masks_of(count):
    masks = []
    while count > 1:
        assert count % 2 == 0
        count //= 2
        masks.append(count)
    return masks


def stages_of(count, stride):
    stages, count = [], count // stride
    while count > 1:
        radix = next(r for r in range(2, count + 1) if count % r == 0)
        stages.append((stride, radix))
        stride, count = stride * radix, count // radix
    return stages


def flip(piece, mask):
    count = lax.axis_size("batch") * lax.axis_size("table")
    return lax.ppermute(piece, ("batch", "table"), [(i ^ mask, i) for i in range(count)])


def turned(piece, stride, radix):
    count = lax.axis_size("batch")
    found = []
    for turn in range(1, radix):
        pairs = []
        for target in range(count):
            digit = target // stride % radix
            pairs.append((target + ((digit + turn) % radix - digit) * stride, target))
        found.append(lax.ppermute(piece, "batch", pairs))
    return found


def sum_stage(total, stride, radix):
    sent = lax.optimization_barrier(total.astype(f16))
    parts = jnp.stack([sent] + turned(sent, stride, radix)) if radix > 2 else None
    if radix > 2:
        digit = lax.axis_index("batch") // stride % radix
        parts = list(parts[(jnp.arange(radix, dtype=jnp.int32) - digit) % radix])
    else:
        parts = [sent] + turned(sent, stride, radix)
    total = parts[0].astype(f32)
    for part in parts[1:]:
        total = total + part.astype(f32)
    return total


def split_parts(rows, terms):
    parts = []
    for _ in range(terms):
        part = lax.reduce_precision(rows, 8, 7)
        parts.append(part.astype(bf16))
        rows = rows - part
    return jnp.concatenate(parts, 1)


def pick_rows(places, blocks, width):
    total, first = None, 0
    for block in blocks:
        count = block.shape[0]
        chosen = (places[:, None] - first == jnp.arange(count, dtype=jnp.int32)[None, :]).astype(bf16)
        found = jnp.dot(chosen, block, preferred_element_type=f32)
        rows = found[:, :width]
        for start in range(width, block.shape[1], width):
            rows = rows + found[:, start : start + width]
        total = rows if total is None else total + rows
        first += count
    return total


def score_piece(query_half, carried, rows, kept):
    total_sum, moment = carried
    scores = score_scale * lax.dot_general(
        query_half, rows, (((1,), (1,)), ((), ())), preferred_element_type=f32
    )
    weights = jnp.where(kept[None, :], jnp.exp(scores), 0.0)
    moment = moment + jnp.dot(weights.astype(bf16), rows, preferred_element_type=f32)
    return (total_sum + jnp.sum(weights, 1), moment)


def score_rows(query_half, rows, kept):
    count, width = rows.shape
    carried = (jnp.zeros(query_half.shape[:1], f32), jnp.zeros(query_half.shape, f32))
    splits = 1
    while count // splits > 1024 and count % (splits * 2) == 0:
        splits = splits * 2
    if splits == 1:
        return score_piece(query_half, carried, rows, kept)
    stacked = (rows.reshape(splits, -1, width), kept.reshape(splits, -1))
    return lax.scan(lambda c, b: (score_piece(query_half, c, *b), None), carried, stacked)[0]


def norm_of(rows):
    return jnp.sqrt(jnp.sum(rows * rows, 1) + epsilon)


def prologue_kernel(fifo, owner, row, head, out):
    queue_rows, width = fifo.shape
    line = lax.broadcasted_iota(jnp.int32, (queue_rows, width), 0)
    lane = lax.broadcasted_iota(jnp.int32, (queue_rows, width), 1)
    told = jnp.full((queue_rows, width), -1, jnp.int32)
    for k in range(ENQ):
        slot = lax.rem(head[0] + k, queue_rows)
        item = jnp.where(lane == 0, owner[0, 0, k], jnp.where(lane == 1, row[0, k] // 16, row[0, k] % 16))
        told = jnp.where(line == slot, item, told)
    block = jnp.concatenate([fifo[...].astype(f32), told.astype(f32)]).astype(bf16)
    out[...] = jnp.broadcast_to(block[None], out.shape)


def one_hot(places, first, count, columns):
    shape = (places.shape[0], count) if columns else (count, places.shape[1])
    numbers = lax.broadcasted_iota(jnp.int32, shape, 1 if columns else 0)
    return (numbers == places - first).astype(f32).astype(bf16)


def split_dot(places, blocks, terms, first=0):
    found = 0.0
    for block in blocks:
        chosen = one_hot(places, first, block.shape[0], True)
        first += block.shape[0]
        rest = block[...]
        for _ in range(terms):
            part = rest.astype(bf16)
            rest = rest - part.astype(f32)
            found = found + jnp.dot(chosen, part, preferred_element_type=f32)
    return found


def unit_of(rows):
    norm = jnp.sqrt(jnp.sum(rows * rows, 1, keepdims=True) + epsilon)
    return rows / norm, norm


def weights_of(unit, negatives):
    scores = lax.dot_general(
        unit.astype(bf16), negatives, (((1,), (1,)), ((), ())), preferred_element_type=f32
    )
    return jnp.exp(score_scale * scores)


def first_kernel(terms, count, queries, places, negatives, *refs):
    blocks, (unit, found, sums) = refs[:count], refs[count:]
    unit[...], _ = unit_of(queries[...].astype(f32))
    found[...] = split_dot(places[...], blocks, terms)
    if negatives.shape[1] > 1:
        sums[...] = jnp.sum(weights_of(unit[...], negatives[...]), 1, keepdims=True)
    else:
        sums[...] = negatives[...]


def main_kernel(step, terms, first, found, block, places, line, queries, negatives, sent, kept, unit):
    item = found[...] + split_dot(places[...], [block], terms, first)
    if step == 0:
        item, _ = unit_of(item)
    unit[...] = item
    query = queries[...]
    if negatives.shape[1] > 1:
        sums = jnp.sum(weights_of(query, negatives[...]), 1, keepdims=True)
    else:
        sums = negatives[...]
    cosine = jnp.sum(query * item, 1, keepdims=True)
    weight = jnp.exp(score_scale * cosine)
    lack = weight / (weight + sums) - 1.0
    rows = (lack * (query - item * cosine)).astype(bf16)
    half = kept.shape[0]
    for out, start in ((sent, half), (kept, 0)):
        chosen = one_hot(line[...], start, half, False)
        out[...] = jnp.dot(chosen, rows, preferred_element_type=f32).astype(out.dtype)


def late_kernel(given, queries, item, negatives, _, *refs):
    query, query_norm = unit_of(queries[...].astype(f32))
    if given:
        (moment_in, loss, grad), sums = refs, negatives[...]
        moment = moment_in[...]
    else:
        loss, grad = refs
        weights = weights_of(query, negatives[...])
        sums = jnp.sum(weights, 1, keepdims=True)
        moment = jnp.dot(weights.astype(bf16), negatives[...], preferred_element_type=f32)
    item = item[...]
    score = score_scale * jnp.sum(query * item, 1, keepdims=True)
    weight = jnp.exp(score)
    total = weight + sums
    loss[...] = jnp.log(total) - score
    unit_grad = score_scale * ((weight / total - 1.0) * item + moment / total)
    along = jnp.sum(query * unit_grad, 1, keepdims=True)
    grad[...] = ((unit_grad - query * along) / query_norm).astype(bf16)


def queue_kernel(terms, count, told, negatives, _, *refs):
    blocks, (out,) = refs[:count], refs[count:]
    item, _ = unit_of(split_dot(told[...], blocks, terms))
    out[...] = jnp.where(told[...] >= 0, item, negatives[...].astype(f32)).astype(bf16)


def update_kernel(scale, side, mine, other, table, accum, _, table_out, accum_out, *unit):
    count = mine.shape[0]
    first = side[...] == 0
    for half, grad in enumerate(((mine, other), (other, mine))):
        place = pl.ds(half * count, count)
        rows = table[place, :]
        _, norm = unit_of(rows)
        grad = jnp.where(first, grad[0][...], grad[1][...]) * (scale / norm)
        moved = accum[place, :] + jnp.mean(grad * grad, 1, keepdims=True)
        accum_out[place, :] = moved
        rows = rows - learn_rate * grad / jnp.sqrt(moved)
        table_out[place, :] = rows
        if unit:
            unit[0][place, :], _ = unit_of(rows)


def call(kernel, outs, *args):
    vmem = pl.BlockSpec(memory_space=pltpu.VMEM)
    return pl.pallas_call(
        kernel,
        out_shape=[jax.ShapeDtypeStruct(shape, dtype) for shape, dtype in outs],
        in_specs=[vmem] * len(args),
        out_specs=[vmem] * len(outs),
        compiler_params=pltpu.CompilerParams(vmem_limit_bytes=20 * 2**20),
    )(*args)


def per_device(queries, item_owner, item_row, table, accum, fifo, fifo_head):
    step_count, query_count, width = queries.shape
    owners, copies = lax.axis_size("table"), lax.axis_size("batch")
    owned = table.shape[0]
    part_rows = owned // 2
    half_rows = owners * owned // 2
    queue_rows = fifo.shape[0]
    me = lax.axis_index("table")
    side = lax.axis_index("batch") % 2
    masks = masks_of(owners)
    small = owners * copies * queue_rows <= 1024
    most = owners * copies * (3 * query_count // owners)
    grad_scale = 1.0
    while most * grad_scale > 32768.0:
        grad_scale = grad_scale / 2

    def owner_place(owner):
        apart = jnp.bitwise_xor(owner, me)
        place = jnp.zeros_like(owner)
        for index, mask in enumerate(masks):
            place = place + jnp.where((apart & mask) != 0, 1 << index, 0)
        return place

    def place_whole(owner, row):
        return owner_place(owner) * owned + row

    def place_part(owner, row):
        return owner_place(owner) * owned + jnp.where(side == 0, row, (row + part_rows) % owned)

    def gather_whole(piece):
        pieces = [piece]
        for mask in masks:
            pieces = pieces + [flip(piece, mask) for piece in pieces]
        return pieces

    def reduce_near(kept):
        pieces = [kept[i * part_rows : (i + 1) * part_rows] for i in range(4)]
        near = [
            flip(piece.astype(f16), mask)
            for piece, mask in zip(pieces[1:], (owners, masks[0], owners + masks[0]))
        ]
        beside = [piece.astype(f32) for piece in near]
        return (pieces[0] + beside[0]) + (beside[1] + beside[2]), near[0][:8].astype(f32)

    def reduce_far(total):
        stages = stages_of(copies, 2)
        for stage in stages[1:]:
            total = sum_stage(total, *stage)
        sent = lax.optimization_barrier(total.astype(f16))
        if stages and stages[0][1] == 2:
            pairs = [[sent, flip(sent, 2 * owners)], [flip(sent, owners), flip(sent, 3 * owners)]]
        else:
            pairs = [[sent], [flip(sent, owners)]]
        return [sum(part.astype(f32) for part in pair) for pair in pairs]

    def next_queue(queue, early):
        if small:
            args = (told, queue, early, *parts)
            return call(functools.partial(queue_kernel, 3, len(parts)), [(queue.shape, bf16)], *args)[0]
        blocks = [split_parts(part, 3) for part in parts]
        new = lax.map(lambda at: pick_rows(at, blocks, width), told.reshape(-1, copies * queue_rows))
        return jnp.where(told >= 0, unit_of(new.reshape(queue.shape))[0].astype(bf16), queue)

    parts, terms = gather_whole(table), 3

    vmem, smem = pl.BlockSpec(memory_space=pltpu.VMEM), pl.BlockSpec(memory_space=pltpu.SMEM)
    blocks = pl.pallas_call(
        prologue_kernel,
        out_shape=jax.ShapeDtypeStruct((owners * copies, 2 * queue_rows, width), bf16),
        in_specs=[vmem, smem, smem, smem],
        out_specs=vmem,
    )(fifo, jnp.transpose(item_owner, (0, 2, 1)), item_row, fifo_head)
    blocks = lax.all_to_all(blocks, ("batch", "table"), 0, 0, tiled=True)
    queue = blocks[:, :queue_rows].reshape(-1, width)
    told = blocks[:, queue_rows:, :3].reshape(-1, 3).astype(jnp.int32)
    replaced = told[:, 0] >= 0
    told = jnp.where(replaced, place_whole(told[:, 0], told[:, 1] * 16 + told[:, 2]), -1)[:, None]

    accum = accum[:, None]
    loss_list, grad_list, joined = [], [], []
    for step in range(step_count):
        places = place_part(item_owner[step, :, 0], item_row[step])
        found_at = place_whole(item_owner[step, :, 0], item_row[step])
        last_place = owners * owned - parts[-1].shape[0]
        parts = [part.astype(f32) for part in parts]
        scalars, matrix = (query_count, 1), (query_count, width)
        if small:
            negatives = queue if step else jnp.zeros(scalars, f32)
        else:
            query_half = unit_of(queries[step].astype(f32))[0].astype(bf16)
            negatives, moment = score_rows(query_half, queue, jnp.ones(queue.shape[:1], jnp.bool_))
            negatives = negatives[:, None]
        query_unit, found, sums = call(
            functools.partial(first_kernel, terms, len(parts) - 1),
            [(matrix, f32), (matrix, f32), (scalars, f32)],
            queries[step],
            found_at[:, None],
            negatives,
            *parts[:-1],
        )
        sent, kept, unit = call(
            functools.partial(main_kernel, step, terms, last_place),
            [((half_rows, width), bf16), ((half_rows, width), f32), (matrix, f32)],
            found,
            parts[-1],
            found_at[:, None],
            places[None, :],
            query_unit,
            queue if small and step == 0 else sums,
        )
        joined.append(unit[:ENQ].astype(bf16))
        sent = (grad_scale * sent).astype(bf16)
        kept = grad_scale * kept
        for mask in masks[:0:-1]:
            kept = kept + flip(sent, mask).astype(f32)
            if mask != masks[1]:
                middle = kept.shape[0] // 2
                kept, sent = kept[:middle], kept[middle:].astype(f16)
        total, early = reduce_near(kept)

        loss, query_grad = call(
            functools.partial(late_kernel, not small),
            [(scalars, f32), (matrix, bf16)],
            queries[step],
            unit,
            queue if small else negatives,
            early,
            *([] if small else [moment]),
        )
        loss_list.append(loss[:, 0])
        grad_list.append(query_grad)
        if step == 0:
            queue = next_queue(queue, early)
        mine, other = reduce_far(total)
        more = step + 1 < step_count
        table, accum, *unit = call(
            functools.partial(update_kernel, score_scale / grad_scale),
            [(table.shape, f32), (accum.shape, f32)] + [(table.shape, f32)] * more,
            jnp.full((1, 1), side),
            mine,
            other,
            table,
            accum,
            queue[:16] if small and more else early,
        )
        if more:
            parts, terms = gather_whole(unit[0].astype(f16)), 2

    slots = jnp.arange(queue_rows, dtype=jnp.int32)
    fifo_out = fifo
    for step in range(step_count):
        place = (slots - fifo_head[0] - step * ENQ) % queue_rows
        for k in range(ENQ):
            fifo_out = jnp.where((place == k)[:, None], joined[step][k][None, :], fifo_out)
    return (jnp.stack(loss_list), jnp.stack(grad_list), table, accum[:, 0], fifo_out)


def solution(mesh):
    both = ("batch", "table")
    in_specs = (
        P(None, both, None),
        P(None, both, None),
        P(None, both),
        P("table", None),
        P("table"),
        P(both, None),
        P(both),
    )
    out_specs = (P(None, both), P(None, both, None), P("table", None), P("table"), P(both, None))
    return jax.shard_map(
        per_device, mesh=mesh, in_specs=in_specs, out_specs=out_specs, check_vma=False
    )
```

```python
import functools

import jax
import jax.numpy as jnp
from jax import lax
from jax.experimental import pallas as pl
from jax.experimental.pallas import tpu as pltpu
from jax.sharding import PartitionSpec as P

ENQ = 4
score_scale = 10.0
learn_rate = 0.3
epsilon = 1e-06
f32 = jnp.float32
bf16 = jnp.bfloat16
f16 = jnp.float16
VMEM = 10 * 2**20


def masks_of(count):
    masks = []
    while count > 1:
        assert count % 2 == 0
        count //= 2
        masks.append(count)
    return masks


def stages_of(count, stride):
    stages, count = [], count // stride
    while count > 1:
        radix = next(r for r in range(2, count + 1) if count % r == 0)
        stages.append((stride, radix))
        stride, count = stride * radix, count // radix
    return stages


def flip(piece, mask):
    count = lax.axis_size("batch") * lax.axis_size("table")
    return lax.ppermute(piece, ("batch", "table"), [(i ^ mask, i) for i in range(count)])


def turned(piece, stride, radix):
    count = lax.axis_size("batch")
    found = []
    for turn in range(1, radix):
        pairs = []
        for target in range(count):
            digit = target // stride % radix
            pairs.append((target + ((digit + turn) % radix - digit) * stride, target))
        found.append(lax.ppermute(piece, "batch", pairs))
    return found


def sum_stage(total, stride, radix, zero=0.0):
    sent = lax.optimization_barrier(total.astype(f16))
    parts = jnp.stack([sent] + turned(sent, stride, radix)) if radix > 2 else None
    if radix > 2:
        digit = lax.axis_index("batch") // stride % radix
        parts = list(parts[(jnp.arange(radix, dtype=jnp.int32) - digit) % radix])
    else:
        parts = [sent] + turned(sent, stride, radix)
    total = parts[0].astype(f32) + zero
    for part in parts[1:]:
        total = total + part.astype(f32)
    return total


def split_parts(rows, terms):
    parts = []
    for _ in range(terms):
        part = lax.reduce_precision(rows, 8, 7)
        parts.append(part.astype(bf16))
        rows = rows - part
    return jnp.concatenate(parts, 1)


def pick_rows(places, blocks, width):
    total, first = None, 0
    for block in blocks:
        count = block.shape[0]
        chosen = (places[:, None] - first == jnp.arange(count, dtype=jnp.int32)[None, :]).astype(bf16)
        found = jnp.dot(chosen, block, preferred_element_type=f32)
        rows = found[:, :width]
        for start in range(width, block.shape[1], width):
            rows = rows + found[:, start : start + width]
        total = rows if total is None else total + rows
        first += count
    return total


def score_piece(query_half, carried, rows, kept):
    total_sum, moment = carried
    scores = score_scale * lax.dot_general(
        query_half, rows, (((1,), (1,)), ((), ())), preferred_element_type=f32
    )
    weights = jnp.where(kept[None, :], jnp.exp(scores), 0.0)
    moment = moment + jnp.dot(weights.astype(bf16), rows, preferred_element_type=f32)
    return (total_sum + jnp.sum(weights, 1), moment)


def score_rows(query_half, rows, kept):
    count, width = rows.shape
    carried = (jnp.zeros(query_half.shape[:1], f32), jnp.zeros(query_half.shape, f32))
    splits = 1
    while count // splits > 1024 and count % (splits * 2) == 0:
        splits = splits * 2
    if splits == 1:
        return score_piece(query_half, carried, rows, kept)
    stacked = (rows.reshape(splits, -1, width), kept.reshape(splits, -1))
    return lax.scan(lambda c, b: (score_piece(query_half, c, *b), None), carried, stacked)[0]


def norm_of(rows):
    return jnp.sqrt(jnp.sum(rows * rows, 1) + epsilon)


def one_hot(places, first, count, columns):
    shape = (places.shape[0], count) if columns else (count, places.shape[1])
    numbers = lax.broadcasted_iota(jnp.int32, shape, 1 if columns else 0)
    return (numbers == places - first).astype(f32).astype(bf16)


def column(line):
    count = line.shape[1]
    tall = jnp.broadcast_to(line, (128, count))
    return jnp.transpose(jnp.pad(tall, ((0, 0), (0, -count % 128))))[:count, :1]


def split_dot(places, blocks, first=0):
    found = 0.0
    for block in blocks:
        count, width = block.shape
        chosen = one_hot(places, first, count, True)
        first += count
        rows = block[...]
        high = rows.astype(bf16)
        low = (rows - high.astype(f32)).astype(bf16)
        both = jnp.concatenate([high, low], 1)
        found = found + jnp.dot(chosen, both, preferred_element_type=f32)
    return found[:, :width] + found[:, width:]


def unit_of(rows):
    norm = jnp.sqrt(jnp.sum(rows * rows, 1, keepdims=True) + epsilon)
    return rows / norm, norm


def weights_of(unit, negatives):
    scores = lax.dot_general(
        unit.astype(bf16), negatives, (((1,), (1,)), ((), ())), preferred_element_type=f32
    )
    return jnp.exp(score_scale * scores)


def told_block(device, owner, row, head, queue_rows, width):
    line = lax.broadcasted_iota(jnp.int32, (queue_rows, width), 0)
    lane = lax.broadcasted_iota(jnp.int32, (queue_rows, width), 1)
    part = jnp.where(lane // 4 == device[...], lane % 4, -1)
    told = jnp.zeros((queue_rows, width), jnp.int32)
    for k in range(ENQ):
        item, number = owner[0, :, k : k + 1], row[0:1, k : k + 1]
        values = jnp.where(part == 0, item + 1, jnp.where(part == 1, number // 16, number % 16))
        values = jnp.where((part >= 0) & (part < 3), values, 0)
        told = jnp.where(line == lax.rem(head[...] + k, queue_rows), values, told)
    return told.astype(f32)


def first_kernel(step, count, scalars, queries, line, negatives, *refs):
    ids, blocks, (unit, found, sums, *told) = refs[:scalars], refs[scalars : scalars + count], refs[scalars + count :]
    unit[...], _ = unit_of(queries[step].astype(f32))
    item = split_dot(column(line[...]), blocks)
    found[...] = unit_of(item)[0] if step == 0 else item
    if negatives.shape[1] > 1:
        sums[...] = jnp.sum(weights_of(unit[...], negatives[...]), 1, keepdims=True)
    else:
        sums[...] = negatives[...]
    if told:
        told[0][...] = told_block(*ids, *told[0].shape)


def main_kernel(first, count, found, found_line, line, queries, negatives, *refs):
    blocks, (told, sent, rows, unit, top) = refs[:count], refs[count:]
    item = found[...]
    if blocks:
        item = item + split_dot(column(found_line[...]), blocks, first)
    unit[...] = item
    top[...] = item[: top.shape[0]]
    query = queries[...]
    if negatives.shape[1] > 1:
        sums = jnp.sum(weights_of(query, negatives[...]), 1, keepdims=True)
    else:
        sums = negatives[...]
    cosine = jnp.sum(query * item, 1, keepdims=True)
    weight = jnp.exp(score_scale * cosine)
    lack = weight / (weight + sums) - 1.0
    rows[...] = (lack * (query - item * cosine)).astype(bf16)
    dense(sent.shape[0], line, rows, told, sent)


def dense(first, line, rows, told, out):
    half, count = out.shape[0], told.shape[0]
    chosen = one_hot(line[...], first, half, False)
    out[...] = jnp.dot(chosen, rows[...], preferred_element_type=f32).astype(out.dtype)
    for end in range(half // 4, half + 1, half // 4):
        out[pl.ds(end - count, count), :] = told[...].astype(out.dtype)


def kept_kernel(line, rows, told, out):
    dense(0, line, rows, told, out)


def late_kernel(step, given, queries, item, negatives, _, *refs):
    query, query_norm = unit_of(queries[step].astype(f32))
    if given:
        moment, sums, refs = refs[0][...], negatives[...], refs[1:]
    else:
        weights = weights_of(query, negatives[...])
        sums = jnp.sum(weights, 1, keepdims=True)
        moment = jnp.dot(weights.astype(bf16), negatives[...], preferred_element_type=f32)
    item = item[...]
    score = score_scale * jnp.sum(query * item, 1, keepdims=True)
    weight = jnp.exp(score)
    total = weight + sums
    loss = jnp.transpose(jnp.broadcast_to(jnp.log(total) - score, item.shape))[:1]
    unit_grad = score_scale * ((weight / total - 1.0) * item + moment / total)
    along = jnp.sum(query * unit_grad, 1, keepdims=True)
    grad = ((unit_grad - query * along) / query_norm).astype(bf16)
    zero, refs = refs[-1], refs[:-1]
    zero[...] = jnp.zeros_like(zero)
    if step == 0:
        fifo, accum, loss_out, grad_out, fifo_out, accum_out = refs
        loss_out[...], grad_out[...] = loss, grad
        fifo_out[...], accum_out[...] = fifo[...], accum[...]
        return
    loss_before, grad_before, fifo, head, *tops, losses, grads, fifo_out = refs
    losses[0:1, :], losses[1:2, :] = loss_before[...], loss
    grads[0], grads[1] = grad_before[...], grad
    queue_rows = fifo.shape[0]
    line = lax.broadcasted_iota(jnp.int32, fifo.shape, 0)
    queue = fifo[...].astype(f32)
    for number, top in enumerate(tops):
        for k in range(ENQ):
            slot = lax.rem(head[...] + (number * ENQ + k), queue_rows)
            queue = jnp.where(line == slot, top[k : k + 1, :], queue)
    fifo_out[...] = queue.astype(bf16)


def queue_kernel(count, told, negatives, *refs):
    blocks, (out, zero) = refs[:count], refs[count:]
    item, _ = unit_of(split_dot(told[...], blocks))
    zero[...] = jnp.zeros_like(zero)
    out[...] = jnp.where(told[...] >= 0, item, negatives[...].astype(f32)).astype(bf16)


def update_kernel(scale, side, mine, other, table, line, table_out, line_out, *unit):
    count = table.shape[0] // 2
    mine, other, first = mine[:count, :], other[:count, :], side[...] == 0
    grad = jnp.concatenate([jnp.where(first, mine, other), jnp.where(first, other, mine)])
    rows = table[...]
    _, norm = unit_of(rows)
    grad = grad * (scale / norm)
    square = grad * grad
    moved = column(line[...]) + jnp.mean(square, 1, keepdims=True)
    ones = jnp.full((8, square.shape[1]), 1.0, f32)
    sums = lax.dot_general(
        ones, square, (((1,), (1,)), ((), ())), precision=lax.Precision.HIGHEST,
        preferred_element_type=f32,
    )
    line_out[...] = line[...] + sums[:1] / square.shape[1]
    rows = rows - learn_rate * grad / jnp.sqrt(moved)
    table_out[...] = rows
    if unit:
        unit[0][...], _ = unit_of(rows)


def call(kernel, outs, *args):
    vmem = pl.BlockSpec(memory_space=pltpu.VMEM)
    return pl.pallas_call(
        kernel,
        out_shape=[jax.ShapeDtypeStruct(shape, dtype) for shape, dtype in outs],
        in_specs=[vmem] * len(args),
        out_specs=[vmem] * len(outs),
        compiler_params=pltpu.CompilerParams(vmem_limit_bytes=VMEM),
    )(*args)


def per_device(queries, item_owner, item_row, table, accum, fifo, fifo_head):
    step_count, query_count, width = queries.shape
    owners, copies = lax.axis_size("table"), lax.axis_size("batch")
    owned = table.shape[0]
    part_rows = owned // 2
    queue_rows = fifo.shape[0]
    devices = owners * copies
    lanes = width // 4
    tiles = -(-devices // lanes)
    stride = part_rows + tiles * queue_rows
    half_rows = owners * stride
    me = lax.axis_index("table")
    side = lax.axis_index("batch") % 2
    masks = masks_of(owners)
    small = devices * queue_rows <= 1024
    most = owners * copies * (3 * query_count // owners)
    grad_scale = 1.0
    while most * grad_scale > 32768.0:
        grad_scale = grad_scale / 2

    def owner_place(owner):
        apart = jnp.bitwise_xor(owner, me)
        place = jnp.zeros_like(owner)
        for index, mask in enumerate(masks):
            place = place + jnp.where((apart & mask) != 0, 1 << index, 0)
        return place

    def place_whole(owner, row):
        return owner_place(owner) * owned + row

    def place_part(owner, row):
        half = row // part_rows
        return (2 * owner_place(owner) + jnp.bitwise_xor(half, side)) * stride + row % part_rows

    def gather_whole(piece):
        pieces = [piece]
        for mask in masks:
            pieces = pieces + [flip(piece, mask) for piece in pieces]
        return pieces

    def reduce_near(kept, came):
        spans = [slice(i * stride, (i + 1) * stride) for i in range(4)]
        pieces = [kept[span] + came[span].astype(f32) for span in spans]
        near = [
            flip(piece.astype(f16), mask)
            for piece, mask in zip(pieces[1:], (owners, masks[0], owners + masks[0]))
        ]
        beside = [piece.astype(f32) for piece in near]
        return (pieces[0] + beside[0]) + (beside[1] + beside[2]), near[0][:8].astype(f32)

    def reduce_far(total, zero):
        stages = stages_of(copies, 2)
        for stage in stages[1:]:
            total = sum_stage(total, *stage, zero)
        sent = lax.optimization_barrier(total.astype(f16))
        if stages and stages[0][1] == 2:
            pairs = [[sent, flip(sent, 2 * owners)], [flip(sent, owners), flip(sent, 3 * owners)]]
        else:
            pairs = [[sent], [flip(sent, owners)]]
        return [sum(part.astype(f32) for part in pair) for pair in pairs]

    def own_told():
        slot = jnp.arange(queue_rows, dtype=jnp.int32)[:, None]
        taken = (slot - fifo_head) % queue_rows == jnp.arange(ENQ, dtype=jnp.int32)
        owner, row = item_owner[0, :ENQ, 0], item_row[0, :ENQ]
        told = [jnp.sum(jnp.where(taken, part, 0), 1) for part in (owner + 1, row // 16, row % 16)]
        told = jnp.stack(told + [jnp.zeros((queue_rows,), jnp.int32)], 1).astype(f32)
        mine = jnp.arange(tiles * lanes, dtype=jnp.int32) == lax.axis_index(("batch", "table"))
        told = jnp.where(mine[:, None, None], told, 0.0).reshape(tiles, lanes, queue_rows, 4)
        return told.transpose(0, 2, 1, 3).reshape(tiles * queue_rows, width)

    def next_queue(queue, told):
        told = (told / grad_scale).reshape(tiles, queue_rows, lanes, 4).transpose(0, 2, 1, 3)
        told = told.reshape(-1, 4)[: devices * queue_rows].astype(jnp.int32)
        place = place_whole(told[:, 0] - 1, told[:, 1] * 16 + told[:, 2])
        place = jnp.where(told[:, 0] > 0, place, -1)[:, None]
        if small:
            kernel = functools.partial(queue_kernel, len(parts))
            queue, zero = call(kernel, [(queue.shape, bf16), (table.shape, f32)], place, queue, *parts)
            return queue, zero
        blocks = [split_parts(part, 2) for part in parts]
        new = lax.map(lambda at: pick_rows(at, blocks, width), place.reshape(-1, copies * queue_rows))
        return jnp.where(place >= 0, unit_of(new.reshape(queue.shape))[0].astype(bf16), queue), 0.0

    parts = gather_whole(table)

    queue = jnp.broadcast_to(jnp.maximum(fifo, bf16(-3e38))[None], (devices, *fifo.shape))
    queue = lax.all_to_all(queue, ("batch", "table"), 0, 0, tiled=True).reshape(-1, width)
    device = jnp.full((1, 1), lax.axis_index(("batch", "table")))

    line = accum[None, :]
    tops = []
    for step in range(step_count):
        places = place_part(item_owner[step, :, 0], item_row[step])
        found_at = place_whole(item_owner[step, :, 0], item_row[step])
        last_place = owners * owned - parts[-1].shape[0]
        parts = [part.astype(f32) for part in parts]
        if step:
            parts[1] = parts[1] + zero
        scalars, matrix = (query_count, 1), (query_count, width)
        if small:
            negatives = queue if step else jnp.zeros(scalars, f32)
        else:
            query_half = unit_of(queries[step].astype(f32))[0].astype(bf16)
            negatives, moment = score_rows(query_half, queue, jnp.ones(queue.shape[:1], jnp.bool_))
            negatives = negatives[:, None]
        split = len(parts) if step == 0 else -1
        ids = [device, jnp.transpose(item_owner, (0, 2, 1)), item_row, fifo_head[None]]
        ids = ids if small and step == 0 else []
        query_unit, found, sums, *own = call(
            functools.partial(first_kernel, step, len(parts[:split]), len(ids)),
            [(matrix, f32), (matrix, f32), (scalars, f32)] + [((queue_rows, width), f32)] * bool(ids),
            queries,
            found_at[None, :],
            negatives,
            *ids,
            *parts[:split],
        )
        if step == 0:
            told = own[0] if own else own_told()
        sent, rows, unit, top = call(
            functools.partial(main_kernel, last_place, len(parts[split:])),
            [((half_rows, width), bf16), (matrix, bf16), (matrix, f32), ((8, width), f32)],
            found,
            found_at[None, :],
            places[None, :],
            query_unit,
            queue if small and step == 0 else sums,
            *parts[split:],
            told,
        )
        tops.append(top)
        (kept,) = call(kept_kernel, [((half_rows, width), f32)], places[None, :], rows, told)
        sent = (grad_scale * sent).astype(bf16)
        kept = grad_scale * kept
        for mask in masks[:1:-1]:
            kept = kept + flip(sent, mask).astype(f32)
            middle = kept.shape[0] // 2
            kept, sent = kept[:middle], kept[middle:].astype(f16)
        total, early = reduce_near(kept, flip(sent, masks[1]))

        more = step + 1 < step_count
        args = [queries, unit, queue if small else negatives, early, *([] if small else [moment])]
        if more:
            outs = [((1, query_count), f32), (matrix, bf16), (fifo.shape, bf16), (line.shape, f32)]
            args += [fifo, line]
        else:
            outs = [((step_count, query_count), f32), (queries.shape, bf16), (fifo.shape, bf16)]
            args += [loss, query_grad, fifo, fifo_head[None], *tops]
        kernel = functools.partial(late_kernel, step, not small)
        loss, query_grad, fifo, *rest, zero = call(kernel, outs + [(total.shape, f32)], *args)
        line = rest[0] if more else line
        mine, other = reduce_far(total, zero)
        table, line, *rest = call(
            functools.partial(update_kernel, score_scale / grad_scale),
            [(table.shape, f32), (line.shape, f32)] + [(table.shape, f32)] * more,
            jnp.full((1, 1), side),
            mine,
            other,
            table,
            line,
        )
        if more:
            queue, zero = next_queue(queue, mine[part_rows:])
            parts = gather_whole(rest[0].astype(f16))

    return (loss, query_grad, table, line[0], fifo)


def solution(mesh):
    both = ("batch", "table")
    in_specs = (
        P(None, both, None),
        P(None, both, None),
        P(None, both),
        P("table", None),
        P("table"),
        P(both, None),
        P(both),
    )
    out_specs = (P(None, both), P(None, both, None), P("table", None), P("table"), P(both, None))
    return jax.shard_map(
        per_device, mesh=mesh, in_specs=in_specs, out_specs=out_specs, check_vma=False
    )
```

```python
import functools

import jax
import jax.numpy as jnp
from jax import lax
from jax.experimental import pallas as pl
from jax.experimental.pallas import tpu as pltpu
from jax.sharding import PartitionSpec as P

ENQ = 4
score_scale = 10.0
learn_rate = 0.3
epsilon = 1e-06
f32 = jnp.float32
bf16 = jnp.bfloat16
f16 = jnp.float16
VMEM = 10 * 2**20


def masks_of(count):
    masks = []
    while count > 1:
        assert count % 2 == 0
        count //= 2
        masks.append(count)
    return masks


def stages_of(count, stride):
    stages, count = [], count // stride
    while count > 1:
        radix = next(r for r in range(2, count + 1) if count % r == 0)
        stages.append((stride, radix))
        stride, count = stride * radix, count // radix
    return stages


def flip(piece, mask):
    count = lax.axis_size("batch") * lax.axis_size("table")
    return lax.ppermute(piece, ("batch", "table"), [(i ^ mask, i) for i in range(count)])


def turned(piece, stride, radix):
    count = lax.axis_size("batch")
    found = []
    for turn in range(1, radix):
        pairs = []
        for target in range(count):
            digit = target // stride % radix
            pairs.append((target + ((digit + turn) % radix - digit) * stride, target))
        found.append(lax.ppermute(piece, "batch", pairs))
    return found


def sum_stage(total, stride, radix, zero=0.0):
    sent = lax.optimization_barrier(total.astype(f16))
    parts = jnp.stack([sent] + turned(sent, stride, radix)) if radix > 2 else None
    if radix > 2:
        digit = lax.axis_index("batch") // stride % radix
        parts = list(parts[(jnp.arange(radix, dtype=jnp.int32) - digit) % radix])
    else:
        parts = [sent] + turned(sent, stride, radix)
    total = parts[0].astype(f32) + zero
    for part in parts[1:]:
        total = total + part.astype(f32)
    return total


def split_parts(rows, terms):
    parts = []
    for _ in range(terms):
        part = lax.reduce_precision(rows, 8, 7)
        parts.append(part.astype(bf16))
        rows = rows - part
    return jnp.concatenate(parts, 1)


def pick_rows(places, blocks, width):
    total, first = None, 0
    for block in blocks:
        count = block.shape[0]
        chosen = (places[:, None] - first == jnp.arange(count, dtype=jnp.int32)[None, :]).astype(bf16)
        found = jnp.dot(chosen, block, preferred_element_type=f32)
        rows = found[:, :width]
        for start in range(width, block.shape[1], width):
            rows = rows + found[:, start : start + width]
        total = rows if total is None else total + rows
        first += count
    return total


def score_piece(query_half, carried, rows, kept):
    total_sum, moment = carried
    scores = score_scale * lax.dot_general(
        query_half, rows, (((1,), (1,)), ((), ())), preferred_element_type=f32
    )
    weights = jnp.where(kept[None, :], jnp.exp(scores), 0.0)
    moment = moment + jnp.dot(weights.astype(bf16), rows, preferred_element_type=f32)
    return (total_sum + jnp.sum(weights, 1), moment)


def score_rows(query_half, rows, kept):
    count, width = rows.shape
    carried = (jnp.zeros(query_half.shape[:1], f32), jnp.zeros(query_half.shape, f32))
    splits = 1
    while count // splits > 1024 and count % (splits * 2) == 0:
        splits = splits * 2
    if splits == 1:
        return score_piece(query_half, carried, rows, kept)
    stacked = (rows.reshape(splits, -1, width), kept.reshape(splits, -1))
    return lax.scan(lambda c, b: (score_piece(query_half, c, *b), None), carried, stacked)[0]


def norm_of(rows):
    return jnp.sqrt(jnp.sum(rows * rows, 1) + epsilon)


def one_hot(places, first, count, columns):
    shape = (places.shape[0], count) if columns else (count, places.shape[1])
    numbers = lax.broadcasted_iota(jnp.int32, shape, 1 if columns else 0)
    return (numbers == places - first).astype(f32).astype(bf16)


def column(line):
    count = line.shape[1]
    tall = jnp.broadcast_to(line, (128, count))
    return jnp.transpose(jnp.pad(tall, ((0, 0), (0, -count % 128))))[:count, :1]


def split_dot(places, blocks, first=0):
    found = 0.0
    for block in blocks:
        count, width = block.shape
        chosen = one_hot(places, first, count, True)
        first += count
        rows = block[...]
        high = rows.astype(bf16)
        low = (rows - high.astype(f32)).astype(bf16)
        both = jnp.concatenate([high, low], 1)
        found = found + jnp.dot(chosen, both, preferred_element_type=f32)
    return found[:, :width] + found[:, width:]


def unit_of(rows):
    norm = jnp.sqrt(jnp.sum(rows * rows, 1, keepdims=True) + epsilon)
    return rows / norm, norm


def weights_of(unit, negatives):
    scores = lax.dot_general(
        unit.astype(bf16), negatives, (((1,), (1,)), ((), ())), preferred_element_type=f32
    )
    return jnp.exp(score_scale * scores)


def told_block(device, owner, row, head, queue_rows, width):
    line = lax.broadcasted_iota(jnp.int32, (queue_rows, width), 0)
    lane = lax.broadcasted_iota(jnp.int32, (queue_rows, width), 1)
    part = jnp.where(lane // 4 == device[...], lane % 4, -1)
    told = jnp.zeros((queue_rows, width), jnp.int32)
    for k in range(ENQ):
        item, number = owner[0, :, k : k + 1], row[0:1, k : k + 1]
        values = jnp.where(part == 0, item + 1, jnp.where(part == 1, number // 16, number % 16))
        values = jnp.where((part >= 0) & (part < 3), values, 0)
        told = jnp.where(line == lax.rem(head[...] + k, queue_rows), values, told)
    return told.astype(f32)


def first_kernel(step, count, scalars, queries, line, negatives, *refs):
    ids, blocks, (unit, found, sums, *told) = refs[:scalars], refs[scalars : scalars + count], refs[scalars + count :]
    unit[...], _ = unit_of(queries[step].astype(f32))
    item = split_dot(column(line[...]), blocks)
    found[...] = unit_of(item)[0] if step == 0 else item
    if negatives.shape[1] > 1:
        sums[...] = jnp.sum(weights_of(unit[...], negatives[...]), 1, keepdims=True)
    else:
        sums[...] = negatives[...]
    if told:
        told[0][...] = told_block(*ids, *told[0].shape)


def main_kernel(first, count, found, found_line, line, queries, negatives, *refs):
    blocks, (told, sent, rows, unit, top) = refs[:count], refs[count:]
    item = found[...]
    if blocks:
        item = item + split_dot(column(found_line[...]), blocks, first)
    unit[...] = item
    top[...] = item[: top.shape[0]]
    query = queries[...]
    if negatives.shape[1] > 1:
        sums = jnp.sum(weights_of(query, negatives[...]), 1, keepdims=True)
    else:
        sums = negatives[...]
    cosine = jnp.sum(query * item, 1, keepdims=True)
    weight = jnp.exp(score_scale * cosine)
    lack = weight / (weight + sums) - 1.0
    rows[...] = (lack * (query - item * cosine)).astype(bf16)
    dense(sent.shape[0], line, rows, told, sent)


def dense(first, line, rows, told, out):
    half, count = out.shape[0], told.shape[0]
    chosen = one_hot(line[...], first, half, False)
    found = jnp.dot(chosen, rows[...], preferred_element_type=f32)
    pieces = []
    for start in range(0, half, half // 4):
        pieces += [found[start : start + half // 4 - count], told[...]]
    out[...] = jnp.concatenate(pieces).astype(out.dtype)


def kept_kernel(line, rows, told, out):
    dense(0, line, rows, told, out)


def widen(line):
    return jnp.pad(line, ((0, 0), (0, -line.shape[1] % 128)))


def shift(line, count):
    return pltpu.roll(line, count % line.shape[1], 1)


def late_kernel(step, given, queries, item, negatives, _, *refs):
    query, query_norm = unit_of(queries[step].astype(f32))
    if given:
        moment, sums, refs = refs[0][...], negatives[...], refs[1:]
    else:
        weights = weights_of(query, negatives[...])
        sums = jnp.sum(weights, 1, keepdims=True)
        moment = jnp.dot(weights.astype(bf16), negatives[...], preferred_element_type=f32)
    item = item[...]
    score = score_scale * jnp.sum(query * item, 1, keepdims=True)
    weight = jnp.exp(score)
    total = weight + sums
    loss = jnp.transpose(jnp.broadcast_to(jnp.log(total) - score, item.shape))[:1]
    unit_grad = score_scale * ((weight / total - 1.0) * item + moment / total)
    along = jnp.sum(query * unit_grad, 1, keepdims=True)
    grad = ((unit_grad - query * along) / query_norm).astype(bf16)
    zero, refs = refs[-1], refs[:-1]
    zero[...] = jnp.zeros_like(zero)
    if step == 0:
        fifo, side, table, accum, loss_out, grad_out, fifo_out, *halves = refs
        loss_out[...], grad_out[...], fifo_out[...] = loss, grad, fifo[...]
        first, count = side[...] == 0, halves[0].shape[0]
        low, high = table[:count, :], table[count:, :]
        halves[0][...], halves[2][...] = jnp.where(first, low, high), jnp.where(first, high, low)
        accum = widen(accum[...])
        low, high = accum[:, :count], shift(accum, -count)[:, :count]
        halves[1][...], halves[3][...] = jnp.where(first, low, high), jnp.where(first, high, low)
        return
    loss_before, grad_before, fifo, head, *tops, losses, grads, fifo_out = refs
    losses[0:1, :], losses[1:2, :] = loss_before[...], loss
    grads[0], grads[1] = grad_before[...], grad
    queue_rows = fifo.shape[0]
    line = lax.broadcasted_iota(jnp.int32, fifo.shape, 0)
    queue = fifo[...].astype(f32)
    for number, top in enumerate(tops):
        for k in range(ENQ):
            slot = lax.rem(head[...] + (number * ENQ + k), queue_rows)
            queue = jnp.where(line == slot, top[k : k + 1, :], queue)
    fifo_out[...] = queue.astype(bf16)


def queue_kernel(count, told, negatives, *refs):
    blocks, (out, zero) = refs[:count], refs[count:]
    item, _ = unit_of(split_dot(told[...], blocks))
    zero[...] = jnp.zeros_like(zero)
    out[...] = jnp.where(told[...] >= 0, item, negatives[...].astype(f32)).astype(bf16)


def adagrad(scale, grad, table, line):
    _, norm = unit_of(table)
    grad = grad * (scale / norm)
    square = grad * grad
    moved = column(line) + jnp.mean(square, 1, keepdims=True)
    ones = jnp.full((8, square.shape[1]), 1.0, f32)
    sums = lax.dot_general(
        ones, square, (((1,), (1,)), ((), ())), precision=lax.Precision.HIGHEST,
        preferred_element_type=f32,
    )
    return table - learn_rate * grad / jnp.sqrt(moved), line + sums[:1] / square.shape[1]


def update_kernel(scale, total, table, line, table_out, line_out, unit):
    rows, line_out[...] = adagrad(scale, total[: table.shape[0], :], table[...], line[...])
    table_out[...] = rows
    unit[...], _ = unit_of(rows)


def finish_kernel(scale, side, mine, other, table, line, far_table, far_line, table_out, line_out):
    count, first = table.shape[0], side[...] == 0

    def in_order(near, far):
        return jnp.concatenate([jnp.where(first, near, far), jnp.where(first, far, near)])

    near, far = widen(line[...]), widen(far_line[...])
    gap = jnp.zeros((1, -(-2 * count // 128) * 128 - near.shape[1]), f32)
    near, far = jnp.concatenate([near, gap], 1), jnp.concatenate([far, gap], 1)
    line = jnp.where(first, near, far) + shift(jnp.where(first, far, near), count)
    grad = in_order(mine[:count, :], other[:count, :])
    rows = in_order(table[...], far_table[...])
    table_out[...], line_out[...] = adagrad(scale, grad, rows, line[:, : 2 * count])


def call(kernel, outs, *args):
    vmem = pl.BlockSpec(memory_space=pltpu.VMEM)
    return pl.pallas_call(
        kernel,
        out_shape=[jax.ShapeDtypeStruct(shape, dtype) for shape, dtype in outs],
        in_specs=[vmem] * len(args),
        out_specs=[vmem] * len(outs),
        compiler_params=pltpu.CompilerParams(vmem_limit_bytes=VMEM),
    )(*args)


def per_device(queries, item_owner, item_row, table, accum, fifo, fifo_head):
    step_count, query_count, width = queries.shape
    owners, copies = lax.axis_size("table"), lax.axis_size("batch")
    owned = table.shape[0]
    part_rows = owned // 2
    queue_rows = fifo.shape[0]
    devices = owners * copies
    lanes = width // 4
    tiles = -(-devices // lanes)
    stride = part_rows + tiles * queue_rows
    half_rows = owners * stride
    me = lax.axis_index("table")
    side = lax.axis_index("batch") % 2
    masks = masks_of(owners)
    small = devices * queue_rows <= 1024 and tiles == 1
    most = owners * copies * (3 * query_count // owners)
    grad_scale = 1.0
    while most * grad_scale > 32768.0:
        grad_scale = grad_scale / 2

    def owner_place(owner):
        apart = jnp.bitwise_xor(owner, me)
        place = jnp.zeros_like(owner)
        for index, mask in enumerate(masks):
            place = place + jnp.where((apart & mask) != 0, 1 << index, 0)
        return place

    def place_whole(owner, row):
        return owner_place(owner) * owned + row

    def place_part(owner, row, stride):
        half = row // part_rows
        return (2 * owner_place(owner) + jnp.bitwise_xor(half, side)) * stride + row % part_rows

    def gather_whole(*pieces):
        pieces = list(pieces)
        for mask in masks:
            pieces = pieces + [flip(piece, mask) for piece in pieces]
        return pieces

    def reduce_near(kept, came):
        spans = [slice(i * stride, (i + 1) * stride) for i in range(4)]
        pieces = [kept[span] + came[span].astype(f32) for span in spans]
        near = [
            flip(piece.astype(f16), mask)
            for piece, mask in zip(pieces[1:], (owners, masks[0], owners + masks[0]))
        ]
        beside = [piece.astype(f32) for piece in near]
        return (pieces[0] + beside[0]) + (beside[1] + beside[2]), near[0][:8].astype(f32)

    def reduce_far(total, zero):
        stages = stages_of(copies, 2)
        paired = stages[:1] == [(2, 2)]
        for stage in stages[paired:]:
            total = sum_stage(total, *stage, zero)
        sent = lax.optimization_barrier(total.astype(f16))
        if paired:
            pairs = [[sent, flip(sent, 2 * owners)], [flip(sent, owners), flip(sent, 3 * owners)]]
        else:
            pairs = [[sent], [flip(sent, owners)]]
        return [sum(part.astype(f32) for part in pair) for pair in pairs]

    def own_told():
        slot = jnp.arange(queue_rows, dtype=jnp.int32)[:, None]
        taken = (slot - fifo_head) % queue_rows == jnp.arange(ENQ, dtype=jnp.int32)
        owner, row = item_owner[0, :ENQ, 0], item_row[0, :ENQ]
        told = [jnp.sum(jnp.where(taken, part, 0), 1) for part in (owner + 1, row // 16, row % 16)]
        told = jnp.stack(told + [jnp.zeros((queue_rows,), jnp.int32)], 1).astype(f32)
        mine = jnp.arange(tiles * lanes, dtype=jnp.int32) == lax.axis_index(("batch", "table"))
        told = jnp.where(mine[:, None, None], told, 0.0).reshape(tiles, lanes, queue_rows, 4)
        return told.transpose(0, 2, 1, 3).reshape(tiles * queue_rows, width)

    def next_queue(queue, told):
        told = (told / grad_scale).reshape(tiles, queue_rows, lanes, 4).transpose(0, 2, 1, 3)
        told = told.reshape(-1, 4)[: devices * queue_rows].astype(jnp.int32)
        place = place_whole(told[:, 0] - 1, told[:, 1] * 16 + told[:, 2])
        place = jnp.where(told[:, 0] > 0, place, -1)[:, None]
        if small:
            kernel = functools.partial(queue_kernel, len(parts))
            queue, zero = call(kernel, [(queue.shape, bf16), ((part_rows, width), f32)], place, queue, *parts)
            return queue, zero
        blocks = [split_parts(part, 2) for part in parts]
        new = lax.map(lambda at: pick_rows(at, blocks, width), place.reshape(-1, copies * queue_rows))
        return jnp.where(place >= 0, unit_of(new.reshape(queue.shape))[0].astype(bf16), queue), 0.0

    parts = gather_whole(table)

    queue = jnp.broadcast_to(jnp.maximum(fifo, bf16(-3e38))[None], (devices, *fifo.shape))
    queue = lax.all_to_all(queue, ("batch", "table"), 0, 0, tiled=True).reshape(-1, width)
    device = jnp.full((1, 1), lax.axis_index(("batch", "table")))

    line = accum[None, :]
    tops = []
    for step in range(step_count):
        owner, row = item_owner[step, :, 0], item_row[step]
        places = place_part(owner, row, stride)
        found_at = place_part(owner, row, part_rows) if step else place_whole(owner, row)
        last_place = owners * owned - parts[-1].shape[0]
        parts = [part.astype(f32) for part in parts]
        if step:
            parts[3] = parts[3] + zero
        scalars, matrix = (query_count, 1), (query_count, width)
        if small:
            negatives = queue if step else jnp.zeros(scalars, f32)
        else:
            query_half = unit_of(queries[step].astype(f32))[0].astype(bf16)
            negatives, moment = score_rows(query_half, queue, jnp.ones(queue.shape[:1], jnp.bool_))
            negatives = negatives[:, None]
        split = len(parts) if step == 0 else -1
        ids = [device, jnp.transpose(item_owner, (0, 2, 1)), item_row, fifo_head[None]]
        ids = ids if small and step == 0 else []
        query_unit, found, sums, *own = call(
            functools.partial(first_kernel, step, len(parts[:split]), len(ids)),
            [(matrix, f32), (matrix, f32), (scalars, f32)] + [((queue_rows, width), f32)] * bool(ids),
            queries,
            found_at[None, :],
            negatives,
            *ids,
            *parts[:split],
        )
        if step == 0:
            told = own[0] if own else own_told()
        sent, rows, unit, top = call(
            functools.partial(main_kernel, last_place, len(parts[split:])),
            [((half_rows, width), bf16), (matrix, bf16), (matrix, f32), ((8, width), f32)],
            found,
            found_at[None, :],
            places[None, :],
            query_unit,
            queue if small and step == 0 else sums,
            *parts[split:],
            told,
        )
        tops.append(top)
        (kept,) = call(kept_kernel, [((half_rows, width), f32)], places[None, :], rows, told)
        sent = (grad_scale * sent).astype(bf16)
        kept = grad_scale * kept
        for mask in masks[:1:-1]:
            kept = kept + flip(sent, mask).astype(f32)
            middle = kept.shape[0] // 2
            kept, sent = kept[:middle], kept[middle:].astype(f16)
        total, early = reduce_near(kept, flip(sent, masks[1]))

        more = step + 1 < step_count
        args = [queries, unit, queue if small else negatives, early, *([] if small else [moment])]
        half_shard = [((part_rows, width), f32), ((1, part_rows), f32)]
        if more:
            outs = [((1, query_count), f32), (matrix, bf16), (fifo.shape, bf16)]
            outs += half_shard + half_shard
            args += [fifo, jnp.full((1, 1), side), table, line]
        else:
            outs = [((step_count, query_count), f32), (queries.shape, bf16), (fifo.shape, bf16)]
            args += [loss, query_grad, fifo, fifo_head[None], *tops]
        kernel = functools.partial(late_kernel, step, not small)
        loss, query_grad, fifo, *rest, zero = call(kernel, outs + [(total.shape, f32)], *args)
        mine, other = reduce_far(total, zero)
        scale = score_scale / grad_scale
        if more:
            kernel, outs = functools.partial(update_kernel, scale), half_shard + half_shard[:1]
            *near, unit = call(kernel, outs, mine, *rest[:2])
            *far, far_unit = call(kernel, outs, other, *rest[2:])
            queue, zero = next_queue(queue, mine[part_rows:])
            parts = gather_whole(unit.astype(f16), far_unit.astype(f16))
        else:
            outs = [(table.shape, f32), (line.shape, f32)]
            args = [jnp.full((1, 1), side), mine, other, *near, *far]
            table, line = call(functools.partial(finish_kernel, scale), outs, *args)

    return (loss, query_grad, table, line[0], fifo)


def solution(mesh):
    both = ("batch", "table")
    in_specs = (
        P(None, both, None),
        P(None, both, None),
        P(None, both),
        P("table", None),
        P("table"),
        P(both, None),
        P(both),
    )
    out_specs = (P(None, both), P(None, both, None), P("table", None), P("table"), P(both, None))
    return jax.shard_map(
        per_device, mesh=mesh, in_specs=in_specs, out_specs=out_specs, check_vma=False
    )
```

```python
import functools

import jax
import jax.numpy as jnp
from jax import lax
from jax.experimental import pallas as pl
from jax.experimental.pallas import tpu as pltpu
from jax.sharding import PartitionSpec as P

ENQ = 4
score_scale = 10.0
learn_rate = 0.3
epsilon = 1e-06
f32 = jnp.float32
bf16 = jnp.bfloat16
f16 = jnp.float16
VMEM = 10 * 2**20


def masks_of(count):
    masks = []
    while count > 1:
        assert count % 2 == 0
        count //= 2
        masks.append(count)
    return masks


def stages_of(count, stride):
    stages, count = [], count // stride
    while count > 1:
        radix = next(r for r in range(2, count + 1) if count % r == 0)
        stages.append((stride, radix))
        stride, count = stride * radix, count // radix
    return stages


def flip(piece, mask):
    count = lax.axis_size("batch") * lax.axis_size("table")
    return lax.ppermute(piece, ("batch", "table"), [(i ^ mask, i) for i in range(count)])


def turned(piece, stride, radix):
    count = lax.axis_size("batch")
    found = []
    for turn in range(1, radix):
        pairs = []
        for target in range(count):
            digit = target // stride % radix
            pairs.append((target + ((digit + turn) % radix - digit) * stride, target))
        found.append(lax.ppermute(piece, "batch", pairs))
    return found


def sum_stage(total, stride, radix, zero=0.0):
    sent = lax.optimization_barrier(total.astype(f16))
    parts = jnp.stack([sent] + turned(sent, stride, radix)) if radix > 2 else None
    if radix > 2:
        digit = lax.axis_index("batch") // stride % radix
        parts = list(parts[(jnp.arange(radix, dtype=jnp.int32) - digit) % radix])
    else:
        parts = [sent] + turned(sent, stride, radix)
    total = parts[0].astype(f32) + zero
    for part in parts[1:]:
        total = total + part.astype(f32)
    return total


def split_parts(rows, terms):
    parts = []
    for _ in range(terms):
        part = lax.reduce_precision(rows, 8, 7)
        parts.append(part.astype(bf16))
        rows = rows - part
    return jnp.concatenate(parts, 1)


def pick_rows(places, blocks, width):
    total, first = None, 0
    for block in blocks:
        count = block.shape[0]
        chosen = (places[:, None] - first == jnp.arange(count, dtype=jnp.int32)[None, :]).astype(bf16)
        found = jnp.dot(chosen, block, preferred_element_type=f32)
        rows = found[:, :width]
        for start in range(width, block.shape[1], width):
            rows = rows + found[:, start : start + width]
        total = rows if total is None else total + rows
        first += count
    return total


def score_piece(query_half, carried, rows, kept):
    total_sum, moment = carried
    scores = score_scale * lax.dot_general(
        query_half, rows, (((1,), (1,)), ((), ())), preferred_element_type=f32
    )
    weights = jnp.where(kept[None, :], jnp.exp(scores), 0.0)
    moment = moment + jnp.dot(weights.astype(bf16), rows, preferred_element_type=f32)
    return (total_sum + jnp.sum(weights, 1), moment)


def score_rows(query_half, rows, kept):
    count, width = rows.shape
    carried = (jnp.zeros(query_half.shape[:1], f32), jnp.zeros(query_half.shape, f32))
    splits = 1
    while count // splits > 1024 and count % (splits * 2) == 0:
        splits = splits * 2
    if splits == 1:
        return score_piece(query_half, carried, rows, kept)
    stacked = (rows.reshape(splits, -1, width), kept.reshape(splits, -1))
    return lax.scan(lambda c, b: (score_piece(query_half, c, *b), None), carried, stacked)[0]


def norm_of(rows):
    return jnp.sqrt(jnp.sum(rows * rows, 1) + epsilon)


def one_hot(places, first, count, columns):
    shape = (places.shape[0], count) if columns else (count, places.shape[1])
    numbers = lax.broadcasted_iota(jnp.int32, shape, 1 if columns else 0)
    return (numbers == places - first).astype(f32).astype(bf16)


def column(line):
    count = line.shape[1]
    tall = jnp.broadcast_to(line, (128, count))
    return jnp.transpose(jnp.pad(tall, ((0, 0), (0, -count % 128))))[:count, :1]


def split_dot(places, blocks, first=0):
    found = 0.0
    for block in blocks:
        count, width = block.shape
        chosen = one_hot(places, first, count, True)
        first += count
        rows = block[...]
        high = rows.astype(bf16)
        low = (rows - high.astype(f32)).astype(bf16)
        both = jnp.concatenate([high, low], 1)
        found = found + jnp.dot(chosen, both, preferred_element_type=f32)
    return found[:, :width] + found[:, width:]


def unit_of(rows):
    norm = jnp.sqrt(jnp.sum(rows * rows, 1, keepdims=True) + epsilon)
    return rows / norm, norm


def weights_of(unit, negatives):
    scores = lax.dot_general(
        unit.astype(bf16), negatives, (((1,), (1,)), ((), ())), preferred_element_type=f32
    )
    return jnp.exp(score_scale * scores)


def told_block(device, owner, row, head, queue_rows, width):
    line = lax.broadcasted_iota(jnp.int32, (queue_rows, width), 0)
    lane = lax.broadcasted_iota(jnp.int32, (queue_rows, width), 1)
    part = jnp.where(lane // 4 == device[...], lane % 4, -1)
    told = jnp.zeros((queue_rows, width), jnp.int32)
    for k in range(ENQ):
        item, number = owner[0, :, k : k + 1], row[0:1, k : k + 1]
        values = jnp.where(part == 0, item + 1, jnp.where(part == 1, number // 16, number % 16))
        values = jnp.where((part >= 0) & (part < 3), values, 0)
        told = jnp.where(line == lax.rem(head[...] + k, queue_rows), values, told)
    return told.astype(f32)


def first_kernel(step, count, scalars, queries, line, negatives, *refs):
    ids, blocks, (unit, found, sums, *told) = refs[:scalars], refs[scalars : scalars + count], refs[scalars + count :]
    unit[...], _ = unit_of(queries[step].astype(f32))
    item = split_dot(column(line[...]), blocks)
    found[...] = unit_of(item)[0] if step == 0 else item
    if negatives.shape[1] > 1:
        sums[...] = jnp.sum(weights_of(unit[...], negatives[...]), 1, keepdims=True)
    else:
        sums[...] = negatives[...]
    if told:
        told[0][...] = told_block(*ids, *told[0].shape)


def main_kernel(first, count, stride, found, found_line, line, queries, negatives, *refs):
    blocks, (told, sent, rows, unit, top) = refs[:count], refs[count:]
    item = found[...]
    if blocks:
        item = item + split_dot(column(found_line[...]), blocks, first)
    unit[...] = item
    top[...] = item[: top.shape[0]]
    query = queries[...]
    if negatives.shape[1] > 1:
        sums = jnp.sum(weights_of(query, negatives[...]), 1, keepdims=True)
    else:
        sums = negatives[...]
    cosine = jnp.sum(query * item, 1, keepdims=True)
    weight = jnp.exp(score_scale * cosine)
    lack = weight / (weight + sums) - 1.0
    rows[...] = (lack * (query - item * cosine)).astype(bf16)
    dense(sent.shape[0], stride, line, rows, told, sent)


def dense(first, stride, line, rows, told, out):
    half, count = out.shape[0], told.shape[0]
    chosen = one_hot(line[...], first, half, False)
    found = jnp.dot(chosen, rows[...], preferred_element_type=f32)
    pieces = []
    for start in range(0, half, stride):
        pieces += [found[start : start + stride - count], told[...]]
    out[...] = jnp.concatenate(pieces).astype(out.dtype)


def kept_kernel(stride, line, rows, told, out):
    dense(0, stride, line, rows, told, out)


def widen(line):
    return jnp.pad(line, ((0, 0), (0, -line.shape[1] % 128)))


def shift(line, count):
    return pltpu.roll(line, count % line.shape[1], 1)


def late_kernel(step, given, queries, item, negatives, _, *refs):
    query, query_norm = unit_of(queries[step].astype(f32))
    if given:
        moment, sums, refs = refs[0][...], negatives[...], refs[1:]
    else:
        weights = weights_of(query, negatives[...])
        sums = jnp.sum(weights, 1, keepdims=True)
        moment = jnp.dot(weights.astype(bf16), negatives[...], preferred_element_type=f32)
    item = item[...]
    score = score_scale * jnp.sum(query * item, 1, keepdims=True)
    weight = jnp.exp(score)
    total = weight + sums
    loss = jnp.transpose(jnp.broadcast_to(jnp.log(total) - score, item.shape))[:1]
    unit_grad = score_scale * ((weight / total - 1.0) * item + moment / total)
    along = jnp.sum(query * unit_grad, 1, keepdims=True)
    grad = ((unit_grad - query * along) / query_norm).astype(bf16)
    zero, refs = refs[-1], refs[:-1]
    zero[...] = jnp.zeros_like(zero)
    if step == 0:
        fifo, side, table, accum, loss_out, grad_out, fifo_out, *halves = refs
        loss_out[...], grad_out[...], fifo_out[...] = loss, grad, fifo[...]
        first, count = side[...] == 0, halves[0].shape[0]
        low, high = table[:count, :], table[count:, :]
        halves[0][...], halves[2][...] = jnp.where(first, low, high), jnp.where(first, high, low)
        accum = widen(accum[...])
        low, high = accum[:, :count], shift(accum, -count)[:, :count]
        halves[1][...], halves[3][...] = jnp.where(first, low, high), jnp.where(first, high, low)
        return
    loss_before, grad_before, fifo, head, *tops, losses, grads, fifo_out = refs
    losses[0:1, :], losses[1:2, :] = loss_before[...], loss
    grads[0], grads[1] = grad_before[...], grad
    queue_rows = fifo.shape[0]
    line = lax.broadcasted_iota(jnp.int32, fifo.shape, 0)
    queue = fifo[...].astype(f32)
    for number, top in enumerate(tops):
        for k in range(ENQ):
            slot = lax.rem(head[...] + (number * ENQ + k), queue_rows)
            queue = jnp.where(line == slot, top[k : k + 1, :], queue)
    fifo_out[...] = queue.astype(bf16)


def queue_kernel(count, told, negatives, *refs):
    blocks, (out, zero) = refs[:count], refs[count:]
    item, _ = unit_of(split_dot(told[...], blocks))
    zero[...] = jnp.zeros_like(zero)
    out[...] = jnp.where(told[...] >= 0, item, negatives[...].astype(f32)).astype(bf16)


def adagrad(scale, grad, table, line):
    _, norm = unit_of(table)
    grad = grad * (scale / norm)
    square = grad * grad
    moved = column(line) + jnp.mean(square, 1, keepdims=True)
    ones = jnp.full((8, square.shape[1]), 1.0, f32)
    sums = lax.dot_general(
        ones, square, (((1,), (1,)), ((), ())), precision=lax.Precision.HIGHEST,
        preferred_element_type=f32,
    )
    return table - learn_rate * grad / jnp.sqrt(moved), line + sums[:1] / square.shape[1]


def update_kernel(scale, total, table, line, table_out, line_out, unit):
    rows, line_out[...] = adagrad(scale, total[: table.shape[0], :], table[...], line[...])
    table_out[...] = rows
    unit[...], _ = unit_of(rows)


def finish_kernel(scale, side, mine, other, table, line, far_table, far_line, table_out, line_out):
    count, first = table.shape[0], side[...] == 0

    def in_order(near, far):
        return jnp.concatenate([jnp.where(first, near, far), jnp.where(first, far, near)])

    near, far = widen(line[...]), widen(far_line[...])
    gap = jnp.zeros((1, -(-2 * count // 128) * 128 - near.shape[1]), f32)
    near, far = jnp.concatenate([near, gap], 1), jnp.concatenate([far, gap], 1)
    line = jnp.where(first, near, far) + shift(jnp.where(first, far, near), count)
    grad = in_order(mine[:count, :], other[:count, :])
    rows = in_order(table[...], far_table[...])
    table_out[...], line_out[...] = adagrad(scale, grad, rows, line[:, : 2 * count])


def call(kernel, outs, *args):
    vmem = pl.BlockSpec(memory_space=pltpu.VMEM)
    return pl.pallas_call(
        kernel,
        out_shape=[jax.ShapeDtypeStruct(shape, dtype) for shape, dtype in outs],
        in_specs=[vmem] * len(args),
        out_specs=[vmem] * len(outs),
        compiler_params=pltpu.CompilerParams(vmem_limit_bytes=VMEM),
    )(*args)


def per_device(queries, item_owner, item_row, table, accum, fifo, fifo_head):
    step_count, query_count, width = queries.shape
    owners, copies = lax.axis_size("table"), lax.axis_size("batch")
    owned = table.shape[0]
    part_rows = owned // 2
    queue_rows = fifo.shape[0]
    devices = owners * copies
    lanes = width // 4
    tiles = -(-devices // lanes)
    stride = part_rows + tiles * queue_rows
    half_rows = owners * stride
    me = lax.axis_index("table")
    side = lax.axis_index("batch") % 2
    masks = masks_of(owners)
    small = devices * queue_rows <= 1024 and tiles == 1
    most = owners * copies * (3 * query_count // owners)
    grad_scale = 1.0
    while most * grad_scale > 32768.0:
        grad_scale = grad_scale / 2

    def owner_place(owner):
        apart = jnp.bitwise_xor(owner, me)
        place = jnp.zeros_like(owner)
        for index, mask in enumerate(masks):
            place = place + jnp.where((apart & mask) != 0, 1 << index, 0)
        return place

    def place_whole(owner, row):
        return owner_place(owner) * owned + row

    def place_part(owner, row, stride):
        half = row // part_rows
        return (2 * owner_place(owner) + jnp.bitwise_xor(half, side)) * stride + row % part_rows

    def gather_whole(*pieces):
        pieces = list(pieces)
        for mask in masks:
            pieces = pieces + [flip(piece, mask) for piece in pieces]
        return pieces

    def reduce_near(kept, came):
        spans = [slice(i * stride, (i + 1) * stride) for i in range(4)]
        pieces = [kept[span] + came[span].astype(f32) for span in spans]
        near = [
            flip(piece.astype(f16), mask)
            for piece, mask in zip(pieces[1:], (owners, masks[0], owners + masks[0]))
        ]
        beside = [piece.astype(f32) for piece in near]
        return (pieces[0] + beside[0]) + (beside[1] + beside[2]), near[0][:8].astype(f32)

    def reduce_far(total, zero):
        stages = stages_of(copies, 2)
        paired = stages[:1] == [(2, 2)]
        for stage in stages[paired:]:
            total = sum_stage(total, *stage, zero)
        sent = lax.optimization_barrier(total.astype(f16))
        if paired:
            pairs = [[sent, flip(sent, 2 * owners)], [flip(sent, owners), flip(sent, 3 * owners)]]
        else:
            pairs = [[sent], [flip(sent, owners)]]
        return [sum(part.astype(f32) for part in pair) for pair in pairs]

    def own_told():
        slot = jnp.arange(queue_rows, dtype=jnp.int32)[:, None]
        taken = (slot - fifo_head) % queue_rows == jnp.arange(ENQ, dtype=jnp.int32)
        owner, row = item_owner[0, :ENQ, 0], item_row[0, :ENQ]
        told = [jnp.sum(jnp.where(taken, part, 0), 1) for part in (owner + 1, row // 16, row % 16)]
        told = jnp.stack(told + [jnp.zeros((queue_rows,), jnp.int32)], 1).astype(f32)
        mine = jnp.arange(tiles * lanes, dtype=jnp.int32) == lax.axis_index(("batch", "table"))
        told = jnp.where(mine[:, None, None], told, 0.0).reshape(tiles, lanes, queue_rows, 4)
        return told.transpose(0, 2, 1, 3).reshape(tiles * queue_rows, width)

    def next_queue(queue, told):
        told = (told / grad_scale).reshape(tiles, queue_rows, lanes, 4).transpose(0, 2, 1, 3)
        told = told.reshape(-1, 4)[: devices * queue_rows].astype(jnp.int32)
        place = place_whole(told[:, 0] - 1, told[:, 1] * 16 + told[:, 2])
        place = jnp.where(told[:, 0] > 0, place, -1)[:, None]
        if small:
            kernel = functools.partial(queue_kernel, len(parts))
            queue, zero = call(kernel, [(queue.shape, bf16), ((part_rows, width), f32)], place, queue, *parts)
            return queue, zero
        blocks = [split_parts(part, 2) for part in parts]
        new = lax.map(lambda at: pick_rows(at, blocks, width), place.reshape(-1, copies * queue_rows))
        return jnp.where(place >= 0, unit_of(new.reshape(queue.shape))[0].astype(bf16), queue), 0.0

    parts = gather_whole(table)

    queue = jnp.broadcast_to(jnp.maximum(fifo, bf16(-3e38))[None], (devices, *fifo.shape))
    queue = lax.all_to_all(queue, ("batch", "table"), 0, 0, tiled=True).reshape(-1, width)
    device = jnp.full((1, 1), lax.axis_index(("batch", "table")))

    line = accum[None, :]
    tops = []
    for step in range(step_count):
        owner, row = item_owner[step, :, 0], item_row[step]
        places = place_part(owner, row, stride)
        found_at = place_part(owner, row, part_rows) if step else place_whole(owner, row)
        last_place = owners * owned - parts[-1].shape[0]
        parts = [part.astype(f32) for part in parts]
        if step:
            parts[3] = parts[3] + zero
        scalars, matrix = (query_count, 1), (query_count, width)
        if small:
            negatives = queue if step else jnp.zeros(scalars, f32)
        else:
            query_half = unit_of(queries[step].astype(f32))[0].astype(bf16)
            negatives, moment = score_rows(query_half, queue, jnp.ones(queue.shape[:1], jnp.bool_))
            negatives = negatives[:, None]
        split = len(parts) if step == 0 else -1
        ids = [device, jnp.transpose(item_owner, (0, 2, 1)), item_row, fifo_head[None]]
        ids = ids if small and step == 0 else []
        query_unit, found, sums, *own = call(
            functools.partial(first_kernel, step, len(parts[:split]), len(ids)),
            [(matrix, f32), (matrix, f32), (scalars, f32)] + [((queue_rows, width), f32)] * bool(ids),
            queries,
            found_at[None, :],
            negatives,
            *ids,
            *parts[:split],
        )
        if step == 0:
            told = own[0] if own else own_told()
        sent, rows, unit, top = call(
            functools.partial(main_kernel, last_place, len(parts[split:]), stride),
            [((half_rows, width), bf16), (matrix, bf16), (matrix, f32), ((8, width), f32)],
            found,
            found_at[None, :],
            places[None, :],
            query_unit,
            queue if small and step == 0 else sums,
            *parts[split:],
            told,
        )
        tops.append(top)
        kernel = functools.partial(kept_kernel, stride)
        (kept,) = call(kernel, [((half_rows, width), f32)], places[None, :], rows, told)
        sent = (grad_scale * sent).astype(bf16)
        kept = grad_scale * kept
        for mask in masks[:1:-1]:
            kept = kept + flip(sent, mask).astype(f32)
            middle = kept.shape[0] // 2
            kept, sent = kept[:middle], kept[middle:].astype(f16)
        total, early = reduce_near(kept, flip(sent, masks[1]))

        more = step + 1 < step_count
        args = [queries, unit, queue if small else negatives, early, *([] if small else [moment])]
        half_shard = [((part_rows, width), f32), ((1, part_rows), f32)]
        if more:
            outs = [((1, query_count), f32), (matrix, bf16), (fifo.shape, bf16)]
            outs += half_shard + half_shard
            args += [fifo, jnp.full((1, 1), side), table, line]
        else:
            outs = [((step_count, query_count), f32), (queries.shape, bf16), (fifo.shape, bf16)]
            args += [loss, query_grad, fifo, fifo_head[None], *tops]
        kernel = functools.partial(late_kernel, step, not small)
        loss, query_grad, fifo, *rest, zero = call(kernel, outs + [(total.shape, f32)], *args)
        mine, other = reduce_far(total, zero)
        scale = score_scale / grad_scale
        if more:
            kernel, outs = functools.partial(update_kernel, scale), half_shard + half_shard[:1]
            *near, unit = call(kernel, outs, mine, *rest[:2])
            *far, far_unit = call(kernel, outs, other, *rest[2:])
            queue, zero = next_queue(queue, mine[part_rows:])
            parts = gather_whole(unit.astype(f16), far_unit.astype(f16))
        else:
            outs = [(table.shape, f32), (line.shape, f32)]
            args = [jnp.full((1, 1), side), mine, other, *near, *far]
            table, line = call(functools.partial(finish_kernel, scale), outs, *args)

    return (loss, query_grad, table, line[0], fifo)


def solution(mesh):
    both = ("batch", "table")
    in_specs = (
        P(None, both, None),
        P(None, both, None),
        P(None, both),
        P("table", None),
        P("table"),
        P(both, None),
        P(both),
    )
    out_specs = (P(None, both), P(None, both, None), P("table", None), P("table"), P(both, None))
    return jax.shard_map(
        per_device, mesh=mesh, in_specs=in_specs, out_specs=out_specs, check_vma=False
    )
```

```python
import functools

import jax
import jax.numpy as jnp
from jax import lax
from jax.experimental import pallas as pl
from jax.experimental.pallas import tpu as pltpu
from jax.sharding import PartitionSpec as P

ENQ = 4
score_scale = 10.0
learn_rate = 0.3
epsilon = 1e-06
f32 = jnp.float32
bf16 = jnp.bfloat16
f16 = jnp.float16
VMEM = 10 * 2**20


def masks_of(count):
    masks = []
    while count > 1:
        assert count % 2 == 0
        count //= 2
        masks.append(count)
    return masks


def stages_of(count, stride):
    stages, count = [], count // stride
    while count > 1:
        radix = next(r for r in range(2, count + 1) if count % r == 0)
        stages.append((stride, radix))
        stride, count = stride * radix, count // radix
    return stages


def flip(piece, mask):
    count = lax.axis_size("batch") * lax.axis_size("table")
    return lax.ppermute(piece, ("batch", "table"), [(i ^ mask, i) for i in range(count)])


def turned(piece, stride, radix):
    count = lax.axis_size("batch")
    found = []
    for turn in range(1, radix):
        pairs = []
        for target in range(count):
            digit = target // stride % radix
            pairs.append((target + ((digit + turn) % radix - digit) * stride, target))
        found.append(lax.ppermute(piece, "batch", pairs))
    return found


def sum_stage(total, stride, radix, zero=0.0):
    sent = lax.optimization_barrier(total.astype(f16))
    parts = jnp.stack([sent] + turned(sent, stride, radix)) if radix > 2 else None
    if radix > 2:
        digit = lax.axis_index("batch") // stride % radix
        parts = list(parts[(jnp.arange(radix, dtype=jnp.int32) - digit) % radix])
    else:
        parts = [sent] + turned(sent, stride, radix)
    total = parts[0].astype(f32) + zero
    for part in parts[1:]:
        total = total + part.astype(f32)
    return total


def split_parts(rows, terms):
    parts = []
    for _ in range(terms):
        part = lax.reduce_precision(rows, 8, 7)
        parts.append(part.astype(bf16))
        rows = rows - part
    return jnp.concatenate(parts, 1)


def pick_rows(places, blocks, width):
    total, first = None, 0
    for block in blocks:
        count = block.shape[0]
        chosen = (places[:, None] - first == jnp.arange(count, dtype=jnp.int32)[None, :]).astype(bf16)
        found = jnp.dot(chosen, block, preferred_element_type=f32)
        rows = found[:, :width]
        for start in range(width, block.shape[1], width):
            rows = rows + found[:, start : start + width]
        total = rows if total is None else total + rows
        first += count
    return total


def score_piece(query_half, carried, rows, kept):
    total_sum, moment = carried
    scores = score_scale * lax.dot_general(
        query_half, rows, (((1,), (1,)), ((), ())), preferred_element_type=f32
    )
    weights = jnp.where(kept[None, :], jnp.exp(scores), 0.0)
    moment = moment + jnp.dot(weights.astype(bf16), rows, preferred_element_type=f32)
    return (total_sum + jnp.sum(weights, 1), moment)


def score_rows(query_half, rows, kept):
    count, width = rows.shape
    carried = (jnp.zeros(query_half.shape[:1], f32), jnp.zeros(query_half.shape, f32))
    splits = 1
    while count // splits > 1024 and count % (splits * 2) == 0:
        splits = splits * 2
    if splits == 1:
        return score_piece(query_half, carried, rows, kept)
    stacked = (rows.reshape(splits, -1, width), kept.reshape(splits, -1))
    return lax.scan(lambda c, b: (score_piece(query_half, c, *b), None), carried, stacked)[0]


def norm_of(rows):
    return jnp.sqrt(jnp.sum(rows * rows, 1) + epsilon)


def one_hot(places, first, count, columns):
    shape = (places.shape[0], count) if columns else (count, places.shape[1])
    numbers = lax.broadcasted_iota(jnp.int32, shape, 1 if columns else 0)
    return (numbers == places - first).astype(f32).astype(bf16)


def column(line):
    count = line.shape[1]
    tall = jnp.broadcast_to(line, (128, count))
    return jnp.transpose(jnp.pad(tall, ((0, 0), (0, -count % 128))))[:count, :1]


def split_dot(places, blocks, first=0):
    found = 0.0
    for block in blocks:
        count, width = block.shape
        chosen = one_hot(places, first, count, True)
        first += count
        rows = block[...]
        high = rows.astype(bf16)
        low = (rows - high.astype(f32)).astype(bf16)
        both = jnp.concatenate([high, low], 1)
        found = found + jnp.dot(chosen, both, preferred_element_type=f32)
    return found[:, :width] + found[:, width:]


def unit_of(rows):
    norm = jnp.sqrt(jnp.sum(rows * rows, 1, keepdims=True) + epsilon)
    return rows / norm, norm


def weights_of(unit, negatives):
    scores = lax.dot_general(
        unit.astype(bf16), negatives, (((1,), (1,)), ((), ())), preferred_element_type=f32
    )
    return jnp.exp(score_scale * scores)


def told_block(device, owner, row, head, queue_rows, width):
    line = lax.broadcasted_iota(jnp.int32, (queue_rows, width), 0)
    lane = lax.broadcasted_iota(jnp.int32, (queue_rows, width), 1)
    part = jnp.where(lane // 4 == device[...], lane % 4, -1)
    told = jnp.zeros((queue_rows, width), jnp.int32)
    for k in range(ENQ):
        item, number = owner[0, :, k : k + 1], row[0:1, k : k + 1]
        values = jnp.where(part == 0, item + 1, jnp.where(part == 1, number // 16, number % 16))
        values = jnp.where((part >= 0) & (part < 3), values, 0)
        told = jnp.where(line == lax.rem(head[...] + k, queue_rows), values, told)
    return told.astype(f32)


def first_kernel(step, count, scalars, queries, line, negatives, *refs):
    ids, blocks, (unit, found, sums, *told) = refs[:scalars], refs[scalars : scalars + count], refs[scalars + count :]
    unit[...], _ = unit_of(queries[step].astype(f32))
    item = split_dot(column(line[...]), blocks)
    found[...] = unit_of(item)[0] if step == 0 else item
    if negatives.shape[1] > 1:
        sums[...] = jnp.sum(weights_of(unit[...], negatives[...]), 1, keepdims=True)
    else:
        sums[...] = negatives[...]
    if told:
        told[0][...] = told_block(*ids, *told[0].shape)


def main_kernel(first, count, stride, found, found_line, line, queries, negatives, *refs):
    blocks, (told, sent, rows, unit, top) = refs[:count], refs[count:]
    item = found[...]
    if blocks:
        item = item + split_dot(column(found_line[...]), blocks, first)
    unit[...] = item
    top[...] = item[: top.shape[0]]
    query = queries[...]
    if negatives.shape[1] > 1:
        sums = jnp.sum(weights_of(query, negatives[...]), 1, keepdims=True)
    else:
        sums = negatives[...]
    cosine = jnp.sum(query * item, 1, keepdims=True)
    weight = jnp.exp(score_scale * cosine)
    lack = weight / (weight + sums) - 1.0
    rows[...] = (lack * (query - item * cosine)).astype(bf16)
    dense(sent.shape[0], stride, line, rows, told, sent)


def dense(first, stride, line, rows, told, out):
    half, count = out.shape[0], told.shape[0]
    chosen = one_hot(line[...], first, half, False)
    found = jnp.dot(chosen, rows[...], preferred_element_type=f32)
    pieces = []
    for start in range(0, half, stride):
        pieces += [found[start : start + stride - count], told[...]]
    out[...] = jnp.concatenate(pieces).astype(out.dtype)


def kept_kernel(stride, line, rows, told, out):
    dense(0, stride, line, rows, told, out)


def late_kernel(step, given, scale, queries, item, negatives, _, *refs):
    query, query_norm = unit_of(queries[step].astype(f32))
    if given:
        moment, sums, refs = refs[0][...], negatives[...], refs[1:]
    else:
        weights = weights_of(query, negatives[...])
        sums = jnp.sum(weights, 1, keepdims=True)
        moment = jnp.dot(weights.astype(bf16), negatives[...], preferred_element_type=f32)
    item = item[...]
    score = score_scale * jnp.sum(query * item, 1, keepdims=True)
    weight = jnp.exp(score)
    total = weight + sums
    loss = jnp.transpose(jnp.broadcast_to(jnp.log(total) - score, item.shape))[:1]
    unit_grad = score_scale * ((weight / total - 1.0) * item + moment / total)
    along = jnp.sum(query * unit_grad, 1, keepdims=True)
    grad = ((unit_grad - query * along) / query_norm).astype(bf16)
    zero, refs = refs[-1], refs[:-1]
    zero[...] = jnp.zeros_like(zero)
    if step == 0:
        fifo, side, table, accum, loss_out, grad_out, fifo_out, *halves = refs
        loss_out[...], grad_out[...], fifo_out[...] = loss, grad, fifo[...]
        rows = table[...]
        values = (rows, column(accum[...]), scale / unit_of(rows)[1])
        first, count = side[...] == 0, halves[0].shape[0]
        for near, far, value in zip(halves[:3], halves[3:], values):
            low, high = value[:count], value[count:]
            near[...], far[...] = jnp.where(first, low, high), jnp.where(first, high, low)
        return
    loss_before, grad_before, fifo, head, *tops, losses, grads, fifo_out = refs
    losses[0:1, :], losses[1:2, :] = loss_before[...], loss
    grads[0], grads[1] = grad_before[...], grad
    queue_rows = fifo.shape[0]
    line = lax.broadcasted_iota(jnp.int32, fifo.shape, 0)
    queue = fifo[...].astype(f32)
    for number, top in enumerate(tops):
        for k in range(ENQ):
            slot = lax.rem(head[...] + (number * ENQ + k), queue_rows)
            queue = jnp.where(line == slot, top[k : k + 1, :], queue)
    fifo_out[...] = queue.astype(bf16)


def queue_kernel(count, told, negatives, *refs):
    blocks, (out, zero) = refs[:count], refs[count:]
    item, _ = unit_of(split_dot(told[...], blocks))
    zero[...] = jnp.zeros_like(zero)
    out[...] = jnp.where(told[...] >= 0, item, negatives[...].astype(f32)).astype(bf16)


def adagrad(grad, table, accum, inverse):
    grad = grad * inverse
    accum = accum + jnp.mean(grad * grad, 1, keepdims=True)
    return table - learn_rate * grad / jnp.sqrt(accum), accum


def update_kernel(scale, total, table, accum, inverse, table_out, accum_out, inverse_out, unit):
    grad = total[: table.shape[0], :]
    rows, accum_out[...] = adagrad(grad, table[...], accum[...], inverse[...])
    table_out[...] = rows
    unit[...], norm = unit_of(rows)
    inverse_out[...] = scale / norm


def finish_kernel(side, mine, other, *refs):
    near, far, (table_out, line_out) = refs[:3], refs[3:6], refs[6:]
    count, first = near[0].shape[0], side[...] == 0

    def in_order(near, far):
        return jnp.concatenate([jnp.where(first, near, far), jnp.where(first, far, near)])

    state = [in_order(a[...], b[...]) for a, b in zip(near, far)]
    rows, accum = adagrad(in_order(mine[:count, :], other[:count, :]), *state)
    table_out[...] = rows
    wide = jnp.pad(accum, ((0, -2 * count % 128), (0, 0)))
    wide = jnp.broadcast_to(wide, (wide.shape[0], 128))
    line_out[...] = jnp.transpose(wide)[:1, : 2 * count]


def call(kernel, outs, *args):
    vmem = pl.BlockSpec(memory_space=pltpu.VMEM)
    return pl.pallas_call(
        kernel,
        out_shape=[jax.ShapeDtypeStruct(shape, dtype) for shape, dtype in outs],
        in_specs=[vmem] * len(args),
        out_specs=[vmem] * len(outs),
        compiler_params=pltpu.CompilerParams(vmem_limit_bytes=VMEM),
    )(*args)


def per_device(queries, item_owner, item_row, table, accum, fifo, fifo_head):
    step_count, query_count, width = queries.shape
    owners, copies = lax.axis_size("table"), lax.axis_size("batch")
    owned = table.shape[0]
    part_rows = owned // 2
    queue_rows = fifo.shape[0]
    devices = owners * copies
    lanes = width // 4
    tiles = -(-devices // lanes)
    stride = part_rows + tiles * queue_rows
    half_rows = owners * stride
    me = lax.axis_index("table")
    side = lax.axis_index("batch") % 2
    masks = masks_of(owners)
    small = devices * queue_rows <= 1024 and tiles == 1
    most = owners * copies * (3 * query_count // owners)
    grad_scale = 1.0
    while most * grad_scale > 32768.0:
        grad_scale = grad_scale / 2

    def owner_place(owner):
        apart = jnp.bitwise_xor(owner, me)
        place = jnp.zeros_like(owner)
        for index, mask in enumerate(masks):
            place = place + jnp.where((apart & mask) != 0, 1 << index, 0)
        return place

    def place_whole(owner, row):
        return owner_place(owner) * owned + row

    def place_part(owner, row, stride):
        half = row // part_rows
        return (2 * owner_place(owner) + jnp.bitwise_xor(half, side)) * stride + row % part_rows

    def gather_whole(*pieces):
        pieces = list(pieces)
        for mask in masks:
            pieces = pieces + [flip(piece, mask) for piece in pieces]
        return pieces

    def reduce_near(kept, came):
        spans = [slice(i * stride, (i + 1) * stride) for i in range(4)]
        pieces = [kept[span] + came[span].astype(f32) for span in spans]
        near = [
            flip(piece.astype(f16), mask)
            for piece, mask in zip(pieces[1:], (owners, masks[0], owners + masks[0]))
        ]
        beside = [piece.astype(f32) for piece in near]
        return (pieces[0] + beside[0]) + (beside[1] + beside[2]), near[0][:8].astype(f32)

    def reduce_far(total, zero):
        stages = stages_of(copies, 2)
        paired = stages[:1] == [(2, 2)]
        for stage in stages[paired:]:
            total = sum_stage(total, *stage, zero)
        sent = lax.optimization_barrier(total.astype(f16))
        if paired:
            pairs = [[sent, flip(sent, 2 * owners)], [flip(sent, owners), flip(sent, 3 * owners)]]
        else:
            pairs = [[sent], [flip(sent, owners)]]
        return [sum(part.astype(f32) for part in pair) for pair in pairs]

    def own_told():
        slot = jnp.arange(queue_rows, dtype=jnp.int32)[:, None]
        taken = (slot - fifo_head) % queue_rows == jnp.arange(ENQ, dtype=jnp.int32)
        owner, row = item_owner[0, :ENQ, 0], item_row[0, :ENQ]
        told = [jnp.sum(jnp.where(taken, part, 0), 1) for part in (owner + 1, row // 16, row % 16)]
        told = jnp.stack(told + [jnp.zeros((queue_rows,), jnp.int32)], 1).astype(f32)
        mine = jnp.arange(tiles * lanes, dtype=jnp.int32) == lax.axis_index(("batch", "table"))
        told = jnp.where(mine[:, None, None], told, 0.0).reshape(tiles, lanes, queue_rows, 4)
        return told.transpose(0, 2, 1, 3).reshape(tiles * queue_rows, width)

    def next_queue(queue, told):
        told = (told / grad_scale).reshape(tiles, queue_rows, lanes, 4).transpose(0, 2, 1, 3)
        told = told.reshape(-1, 4)[: devices * queue_rows].astype(jnp.int32)
        place = place_whole(told[:, 0] - 1, told[:, 1] * 16 + told[:, 2])
        place = jnp.where(told[:, 0] > 0, place, -1)[:, None]
        if small:
            kernel = functools.partial(queue_kernel, len(parts))
            queue, zero = call(kernel, [(queue.shape, bf16), ((part_rows, width), f32)], place, queue, *parts)
            return queue, zero
        blocks = [split_parts(part, 2) for part in parts]
        new = lax.map(lambda at: pick_rows(at, blocks, width), place.reshape(-1, copies * queue_rows))
        return jnp.where(place >= 0, unit_of(new.reshape(queue.shape))[0].astype(bf16), queue), 0.0

    parts = gather_whole(table)

    queue = jnp.broadcast_to(jnp.maximum(fifo, bf16(-3e38))[None], (devices, *fifo.shape))
    queue = lax.all_to_all(queue, ("batch", "table"), 0, 0, tiled=True).reshape(-1, width)
    device = jnp.full((1, 1), lax.axis_index(("batch", "table")))

    line = accum[None, :]
    tops = []
    for step in range(step_count):
        owner, row = item_owner[step, :, 0], item_row[step]
        places = place_part(owner, row, stride)
        found_at = place_part(owner, row, part_rows) if step else place_whole(owner, row)
        last_place = owners * owned - parts[-1].shape[0]
        parts = [part.astype(f32) for part in parts]
        if step:
            parts[3] = parts[3] + zero
        scalars, matrix = (query_count, 1), (query_count, width)
        if small:
            negatives = queue if step else jnp.zeros(scalars, f32)
        else:
            query_half = unit_of(queries[step].astype(f32))[0].astype(bf16)
            negatives, moment = score_rows(query_half, queue, jnp.ones(queue.shape[:1], jnp.bool_))
            negatives = negatives[:, None]
        split = len(parts) if step == 0 else -1
        ids = [device, jnp.transpose(item_owner, (0, 2, 1)), item_row, fifo_head[None]]
        ids = ids if small and step == 0 else []
        query_unit, found, sums, *own = call(
            functools.partial(first_kernel, step, len(parts[:split]), len(ids)),
            [(matrix, f32), (matrix, f32), (scalars, f32)] + [((queue_rows, width), f32)] * bool(ids),
            queries,
            found_at[None, :],
            negatives,
            *ids,
            *parts[:split],
        )
        if step == 0:
            told = own[0] if own else own_told()
        sent, rows, unit, top = call(
            functools.partial(main_kernel, last_place, len(parts[split:]), stride),
            [((half_rows, width), bf16), (matrix, bf16), (matrix, f32), ((8, width), f32)],
            found,
            found_at[None, :],
            places[None, :],
            query_unit,
            queue if small and step == 0 else sums,
            *parts[split:],
            told,
        )
        tops.append(top)
        kernel = functools.partial(kept_kernel, stride)
        (kept,) = call(kernel, [((half_rows, width), f32)], places[None, :], rows, told)
        sent = (grad_scale * sent).astype(bf16)
        kept = grad_scale * kept
        for mask in masks[:1:-1]:
            kept = kept + flip(sent, mask).astype(f32)
            middle = kept.shape[0] // 2
            kept, sent = kept[:middle], kept[middle:].astype(f16)
        total, early = reduce_near(kept, flip(sent, masks[1]))

        more = step + 1 < step_count
        args = [queries, unit, queue if small else negatives, early, *([] if small else [moment])]
        scalar = ((part_rows, 1), f32)
        half_shard = [((part_rows, width), f32), scalar, scalar]
        scale = score_scale / grad_scale
        if more:
            outs = [((1, query_count), f32), (matrix, bf16), (fifo.shape, bf16)]
            outs += half_shard + half_shard
            args += [fifo, jnp.full((1, 1), side), table, line]
        else:
            outs = [((step_count, query_count), f32), (queries.shape, bf16), (fifo.shape, bf16)]
            args += [loss, query_grad, fifo, fifo_head[None], *tops]
        kernel = functools.partial(late_kernel, step, not small, scale)
        loss, query_grad, fifo, *rest, zero = call(kernel, outs + [(total.shape, f32)], *args)
        mine, other = reduce_far(total, zero)
        if more:
            kernel, outs = functools.partial(update_kernel, scale), half_shard + half_shard[:1]
            *near, unit = call(kernel, outs, mine, *rest[:3])
            *far, far_unit = call(kernel, outs, other, *rest[3:])
            queue, zero = next_queue(queue, mine[part_rows:])
            parts = gather_whole(unit.astype(f16), far_unit.astype(f16))
        else:
            outs = [(table.shape, f32), (line.shape, f32)]
            args = [jnp.full((1, 1), side), mine, other, *near, *far]
            table, line = call(finish_kernel, outs, *args)

    return (loss, query_grad, table, line[0], fifo)


def solution(mesh):
    both = ("batch", "table")
    in_specs = (
        P(None, both, None),
        P(None, both, None),
        P(None, both),
        P("table", None),
        P("table"),
        P(both, None),
        P(both),
    )
    out_specs = (P(None, both), P(None, both, None), P("table", None), P("table"), P(both, None))
    return jax.shard_map(
        per_device, mesh=mesh, in_specs=in_specs, out_specs=out_specs, check_vma=False
    )
```

```python
import functools

import jax
import jax.numpy as jnp
from jax import lax
from jax.experimental import pallas as pl
from jax.experimental.pallas import tpu as pltpu
from jax.sharding import PartitionSpec as P

ENQ = 4
score_scale = 10.0
learn_rate = 0.3
epsilon = 1e-06
f32 = jnp.float32
bf16 = jnp.bfloat16
f16 = jnp.float16
VMEM = 10 * 2**20


def masks_of(count):
    masks = []
    while count > 1:
        assert count % 2 == 0
        count //= 2
        masks.append(count)
    return masks


def stages_of(count, stride):
    stages, count = [], count // stride
    while count > 1:
        radix = next(r for r in range(2, count + 1) if count % r == 0)
        stages.append((stride, radix))
        stride, count = stride * radix, count // radix
    return stages


def flip(piece, mask):
    count = lax.axis_size("batch") * lax.axis_size("table")
    return lax.ppermute(piece, ("batch", "table"), [(i ^ mask, i) for i in range(count)])


def turned(piece, stride, radix):
    count = lax.axis_size("batch")
    found = []
    for turn in range(1, radix):
        pairs = []
        for target in range(count):
            digit = target // stride % radix
            pairs.append((target + ((digit + turn) % radix - digit) * stride, target))
        found.append(lax.ppermute(piece, "batch", pairs))
    return found


def sum_stage(total, stride, radix, zero=0.0):
    sent = lax.optimization_barrier(total.astype(f16))
    parts = jnp.stack([sent] + turned(sent, stride, radix)) if radix > 2 else None
    if radix > 2:
        digit = lax.axis_index("batch") // stride % radix
        parts = list(parts[(jnp.arange(radix, dtype=jnp.int32) - digit) % radix])
    else:
        parts = [sent] + turned(sent, stride, radix)
    total = parts[0].astype(f32) + zero
    for part in parts[1:]:
        total = total + part.astype(f32)
    return total


def split_parts(rows, terms):
    parts = []
    for _ in range(terms):
        part = lax.reduce_precision(rows, 8, 7)
        parts.append(part.astype(bf16))
        rows = rows - part
    return jnp.concatenate(parts, 1)


def pick_rows(places, blocks, width):
    total, first = None, 0
    for block in blocks:
        count = block.shape[0]
        chosen = (places[:, None] - first == jnp.arange(count, dtype=jnp.int32)[None, :]).astype(bf16)
        found = jnp.dot(chosen, block, preferred_element_type=f32)
        rows = found[:, :width]
        for start in range(width, block.shape[1], width):
            rows = rows + found[:, start : start + width]
        total = rows if total is None else total + rows
        first += count
    return total


def score_piece(query_half, carried, rows, kept):
    total_sum, moment = carried
    scores = score_scale * lax.dot_general(
        query_half, rows, (((1,), (1,)), ((), ())), preferred_element_type=f32
    )
    weights = jnp.where(kept[None, :], jnp.exp(scores), 0.0)
    moment = moment + jnp.dot(weights.astype(bf16), rows, preferred_element_type=f32)
    return (total_sum + jnp.sum(weights, 1), moment)


def score_rows(query_half, rows, kept):
    count, width = rows.shape
    carried = (jnp.zeros(query_half.shape[:1], f32), jnp.zeros(query_half.shape, f32))
    splits = 1
    while count // splits > 1024 and count % (splits * 2) == 0:
        splits = splits * 2
    if splits == 1:
        return score_piece(query_half, carried, rows, kept)
    stacked = (rows.reshape(splits, -1, width), kept.reshape(splits, -1))
    return lax.scan(lambda c, b: (score_piece(query_half, c, *b), None), carried, stacked)[0]


def norm_of(rows):
    return jnp.sqrt(jnp.sum(rows * rows, 1) + epsilon)


def one_hot(places, first, count, columns):
    shape = (places.shape[0], count) if columns else (count, places.shape[1])
    numbers = lax.broadcasted_iota(jnp.int32, shape, 1 if columns else 0)
    return (numbers == places - first).astype(f32).astype(bf16)


def column(line):
    count = line.shape[1]
    tall = jnp.broadcast_to(line, (128, count))
    return jnp.transpose(jnp.pad(tall, ((0, 0), (0, -count % 128))))[:count, :1]


def split_dot(places, blocks, first=0):
    found = 0.0
    for block in blocks:
        count, width = block.shape
        chosen = one_hot(places, first, count, True)
        first += count
        rows = block[...]
        high = rows.astype(bf16)
        low = (rows - high.astype(f32)).astype(bf16)
        both = jnp.concatenate([high, low], 1)
        found = found + jnp.dot(chosen, both, preferred_element_type=f32)
    return found[:, :width] + found[:, width:]


def unit_of(rows):
    norm = jnp.sqrt(jnp.sum(rows * rows, 1, keepdims=True) + epsilon)
    return rows / norm, norm


def weights_of(unit, negatives):
    scores = lax.dot_general(
        unit.astype(bf16), negatives, (((1,), (1,)), ((), ())), preferred_element_type=f32
    )
    return jnp.exp(score_scale * scores)


def told_block(device, owner, row, head, queue_rows, width):
    line = lax.broadcasted_iota(jnp.int32, (queue_rows, width), 0)
    lane = lax.broadcasted_iota(jnp.int32, (queue_rows, width), 1)
    part = jnp.where(lane // 4 == device[...], lane % 4, -1)
    told = jnp.zeros((queue_rows, width), jnp.int32)
    for k in range(ENQ):
        item, number = owner[0, :, k : k + 1], row[0:1, k : k + 1]
        values = jnp.where(part == 0, item + 1, jnp.where(part == 1, number // 16, number % 16))
        values = jnp.where((part >= 0) & (part < 3), values, 0)
        told = jnp.where(line == lax.rem(head[...] + k, queue_rows), values, told)
    return told.astype(f32)


def first_kernel(step, count, scalars, queries, line, negatives, *refs):
    ids, blocks, refs = refs[:scalars], refs[scalars : scalars + count], refs[scalars + count :]
    if step == 0:
        places, unit, found, sums, *told = refs
        told = (places, *told)
    else:
        unit, found, sums = refs
    unit[...], _ = unit_of(queries[step].astype(f32))
    item = split_dot(column(line[...]), blocks)
    found[...] = unit_of(item)[0] if step == 0 else item
    if negatives.shape[1] > 1:
        sums[...] = jnp.sum(weights_of(unit[...], negatives[...]), 1, keepdims=True)
    else:
        sums[...] = negatives[...]
    if step == 0:
        places, away, half, notes, top, *told = told
        query, item = unit[...], found[...]
        cosine = jnp.sum(query * item, 1, keepdims=True)
        away[...] = (query - item * cosine).astype(bf16)
        half[...] = query.astype(bf16)
        spread = jnp.broadcast_to(score_scale * cosine, item.shape)
        weight = jnp.exp(jnp.transpose(spread)[:1])
        line = places[...].astype(f32)
        notes[:8, :] = jnp.concatenate([weight, line, jnp.zeros((6, line.shape[1]), f32)])
        top[...] = item[: top.shape[0]]
        if told:
            block = told_block(*ids, *told[0].shape)
            told[0][...] = block
            gap = jnp.zeros((block.shape[0], line.shape[1] - block.shape[1]), f32)
            notes[8:, :] = jnp.concatenate([block, gap], 1)


def main_kernel(first, count, stride, found, found_line, line, queries, negatives, *refs):
    blocks, (told, sent, rows, unit, top) = refs[:count], refs[count:]
    item = found[...]
    if blocks:
        item = item + split_dot(column(found_line[...]), blocks, first)
    unit[...] = item
    top[...] = item[: top.shape[0]]
    query = queries[...]
    if negatives.shape[1] > 1:
        sums = jnp.sum(weights_of(query, negatives[...]), 1, keepdims=True)
    else:
        sums = negatives[...]
    cosine = jnp.sum(query * item, 1, keepdims=True)
    weight = jnp.exp(score_scale * cosine)
    lack = weight / (weight + sums) - 1.0
    rows[...] = (lack * (query - item * cosine)).astype(bf16)
    dense(sent.shape[0], stride, line, rows, told, sent)


def dense_rows(first, half, stride, line, rows, told, lack=1.0):
    count = told.shape[0]
    numbers = lax.broadcasted_iota(jnp.int32, (half, rows.shape[0]), 0)
    chosen = jnp.where(numbers == line - first, lack, 0.0).astype(bf16)
    found = jnp.dot(chosen, rows, preferred_element_type=f32)
    pieces = []
    for start in range(0, half, stride):
        pieces += [found[start : start + stride - count], told]
    return jnp.concatenate(pieces)


def dense(first, stride, line, rows, told, out):
    found = dense_rows(first, out.shape[0], stride, line[...], rows[...], told[...])
    out[...] = found.astype(out.dtype)


def start_kernel(stride, far, away, half, notes, told, negatives, *refs):
    out = refs[-1]
    if negatives.dtype == bf16:
        scores = lax.dot_general(
            negatives[...], half[...], (((1,), (1,)), ((), ())), preferred_element_type=f32
        )
        sums = jnp.sum(jnp.exp(score_scale * scores), 0, keepdims=True)
    else:
        sums = negatives[...]
    weight, line = notes[0:1, :], notes[1:2, :].astype(jnp.int32)
    lack = weight / (weight + sums) - 1.0
    count = out.shape[0]
    rows = dense_rows(count if far else 0, count, stride, line, away[...], told[...], lack)
    out[...] = rows + refs[0][...] if far else rows


def kept_kernel(stride, line, rows, told, out):
    dense(0, stride, line, rows, told, out)


def late_kernel(step, given, scale, queries, item, negatives, _, *refs):
    query, query_norm = unit_of(queries[step].astype(f32))
    if given:
        moment, sums, refs = refs[0][...], negatives[...], refs[1:]
    else:
        weights = weights_of(query, negatives[...])
        sums = jnp.sum(weights, 1, keepdims=True)
        moment = jnp.dot(weights.astype(bf16), negatives[...], preferred_element_type=f32)
    item = item[...]
    score = score_scale * jnp.sum(query * item, 1, keepdims=True)
    weight = jnp.exp(score)
    total = weight + sums
    loss = jnp.transpose(jnp.broadcast_to(jnp.log(total) - score, item.shape))[:1]
    unit_grad = score_scale * ((weight / total - 1.0) * item + moment / total)
    along = jnp.sum(query * unit_grad, 1, keepdims=True)
    grad = ((unit_grad - query * along) / query_norm).astype(bf16)
    zero, refs = refs[-1], refs[:-1]
    zero[...] = jnp.zeros_like(zero)
    if step == 0:
        fifo, side, table, accum, loss_out, grad_out, fifo_out, *halves = refs
        loss_out[...], grad_out[...], fifo_out[...] = loss, grad, fifo[...]
        rows = table[...]
        values = (rows, column(accum[...]), scale / unit_of(rows)[1])
        first, count = side[...] == 0, halves[0].shape[0]
        for near, far, value in zip(halves[:3], halves[3:], values):
            low, high = value[:count], value[count:]
            near[...], far[...] = jnp.where(first, low, high), jnp.where(first, high, low)
        return
    loss_before, grad_before, fifo, head, *tops, losses, grads, fifo_out = refs
    losses[0:1, :], losses[1:2, :] = loss_before[...], loss
    grads[0], grads[1] = grad_before[...], grad
    queue_rows = fifo.shape[0]
    line = lax.broadcasted_iota(jnp.int32, fifo.shape, 0)
    queue = fifo[...].astype(f32)
    for number, top in enumerate(tops):
        for k in range(ENQ):
            slot = lax.rem(head[...] + (number * ENQ + k), queue_rows)
            queue = jnp.where(line == slot, top[k : k + 1, :], queue)
    fifo_out[...] = queue.astype(bf16)


def queue_kernel(count, told, negatives, *refs):
    blocks, (out, zero) = refs[:count], refs[count:]
    item, _ = unit_of(split_dot(told[...], blocks))
    zero[...] = jnp.zeros_like(zero)
    out[...] = jnp.where(told[...] >= 0, item, negatives[...].astype(f32)).astype(bf16)


def adagrad(grad, table, accum, inverse):
    grad = grad * inverse
    accum = accum + jnp.mean(grad * grad, 1, keepdims=True)
    return table - learn_rate * grad / jnp.sqrt(accum), accum


def update_kernel(scale, total, table, accum, inverse, table_out, accum_out, inverse_out, unit):
    grad = total[: table.shape[0], :]
    rows, accum_out[...] = adagrad(grad, table[...], accum[...], inverse[...])
    table_out[...] = rows
    unit[...], norm = unit_of(rows)
    inverse_out[...] = scale / norm


def finish_kernel(side, mine, other, *refs):
    near, far, (table_out, line_out) = refs[:3], refs[3:6], refs[6:]
    count, first = near[0].shape[0], side[...] == 0

    def in_order(near, far):
        return jnp.concatenate([jnp.where(first, near, far), jnp.where(first, far, near)])

    state = [in_order(a[...], b[...]) for a, b in zip(near, far)]
    rows, accum = adagrad(in_order(mine[:count, :], other[:count, :]), *state)
    table_out[...] = rows
    wide = jnp.pad(accum, ((0, -2 * count % 128), (0, 0)))
    wide = jnp.broadcast_to(wide, (wide.shape[0], 128))
    line_out[...] = jnp.transpose(wide)[:1, : 2 * count]


def call(kernel, outs, *args):
    vmem = pl.BlockSpec(memory_space=pltpu.VMEM)
    return pl.pallas_call(
        kernel,
        out_shape=[jax.ShapeDtypeStruct(shape, dtype) for shape, dtype in outs],
        in_specs=[vmem] * len(args),
        out_specs=[vmem] * len(outs),
        compiler_params=pltpu.CompilerParams(vmem_limit_bytes=VMEM),
    )(*args)


def per_device(queries, item_owner, item_row, table, accum, fifo, fifo_head):
    step_count, query_count, width = queries.shape
    owners, copies = lax.axis_size("table"), lax.axis_size("batch")
    owned = table.shape[0]
    part_rows = owned // 2
    queue_rows = fifo.shape[0]
    devices = owners * copies
    lanes = width // 4
    tiles = -(-devices // lanes)
    stride = part_rows + tiles * queue_rows
    half_rows = owners * stride
    me = lax.axis_index("table")
    side = lax.axis_index("batch") % 2
    masks = masks_of(owners)
    small = devices * queue_rows <= 1024 and tiles == 1
    most = owners * copies * (3 * query_count // owners)
    grad_scale = 1.0
    while most * grad_scale > 32768.0:
        grad_scale = grad_scale / 2

    def owner_place(owner):
        apart = jnp.bitwise_xor(owner, me)
        place = jnp.zeros_like(owner)
        for index, mask in enumerate(masks):
            place = place + jnp.where((apart & mask) != 0, 1 << index, 0)
        return place

    def place_whole(owner, row):
        return owner_place(owner) * owned + row

    def place_part(owner, row, stride):
        half = row // part_rows
        return (2 * owner_place(owner) + jnp.bitwise_xor(half, side)) * stride + row % part_rows

    def gather_whole(*pieces):
        pieces = list(pieces)
        for mask in masks:
            pieces = pieces + [flip(piece, mask) for piece in pieces]
        return pieces

    def reduce_near(kept, came=None):
        spans = [slice(i * stride, (i + 1) * stride) for i in range(4)]
        pieces = [kept[span] for span in spans]
        if came is not None:
            pieces = [piece + came[span].astype(f32) for piece, span in zip(pieces, spans)]
        near = [
            flip(piece.astype(f16), mask)
            for piece, mask in zip(pieces[1:], (owners, masks[0], owners + masks[0]))
        ]
        beside = [piece.astype(f32) for piece in near]
        return (pieces[0] + beside[0]) + (beside[1] + beside[2]), near[0][:8].astype(f32)

    def reduce_far(total, zero):
        stages = stages_of(copies, 2)
        paired = stages[:1] == [(2, 2)]
        for stage in stages[paired:]:
            total = sum_stage(total, *stage, zero)
        sent = lax.optimization_barrier(total.astype(f16))
        if paired:
            pairs = [[sent, flip(sent, 2 * owners)], [flip(sent, owners), flip(sent, 3 * owners)]]
        else:
            pairs = [[sent], [flip(sent, owners)]]
        return [sum(part.astype(f32) for part in pair) for pair in pairs]

    def own_told():
        slot = jnp.arange(queue_rows, dtype=jnp.int32)[:, None]
        taken = (slot - fifo_head) % queue_rows == jnp.arange(ENQ, dtype=jnp.int32)
        owner, row = item_owner[0, :ENQ, 0], item_row[0, :ENQ]
        told = [jnp.sum(jnp.where(taken, part, 0), 1) for part in (owner + 1, row // 16, row % 16)]
        told = jnp.stack(told + [jnp.zeros((queue_rows,), jnp.int32)], 1).astype(f32)
        mine = jnp.arange(tiles * lanes, dtype=jnp.int32) == lax.axis_index(("batch", "table"))
        told = jnp.where(mine[:, None, None], told, 0.0).reshape(tiles, lanes, queue_rows, 4)
        return told.transpose(0, 2, 1, 3).reshape(tiles * queue_rows, width)

    def next_queue(queue, told):
        told = (told / grad_scale).reshape(tiles, queue_rows, lanes, 4).transpose(0, 2, 1, 3)
        told = told.reshape(-1, 4)[: devices * queue_rows].astype(jnp.int32)
        place = place_whole(told[:, 0] - 1, told[:, 1] * 16 + told[:, 2])
        place = jnp.where(told[:, 0] > 0, place, -1)[:, None]
        if small:
            kernel = functools.partial(queue_kernel, len(parts))
            queue, zero = call(kernel, [(queue.shape, bf16), ((part_rows, width), f32)], place, queue, *parts)
            return queue, zero
        blocks = [split_parts(part, 2) for part in parts]
        new = lax.map(lambda at: pick_rows(at, blocks, width), place.reshape(-1, copies * queue_rows))
        return jnp.where(place >= 0, unit_of(new.reshape(queue.shape))[0].astype(bf16), queue), 0.0

    parts = gather_whole(table)

    queue = jnp.broadcast_to(jnp.maximum(fifo, bf16(-3e38))[None], (devices, *fifo.shape))
    queue = lax.all_to_all(queue, ("batch", "table"), 0, 0, tiled=True).reshape(-1, width)
    device = jnp.full((1, 1), lax.axis_index(("batch", "table")))

    line = accum[None, :]
    tops = []
    for step in range(step_count):
        owner, row = item_owner[step, :, 0], item_row[step]
        places = place_part(owner, row, stride)
        found_at = place_part(owner, row, part_rows) if step else place_whole(owner, row)
        last_place = owners * owned - parts[-1].shape[0]
        parts = [part.astype(f32) for part in parts]
        if step:
            parts[3] = parts[3] + zero
        scalars, matrix = (query_count, 1), (query_count, width)
        if small:
            negatives = queue if step else jnp.zeros(scalars, f32)
        else:
            query_half = unit_of(queries[step].astype(f32))[0].astype(bf16)
            negatives, moment = score_rows(query_half, queue, jnp.ones(queue.shape[:1], jnp.bool_))
            negatives = negatives[:, None]
        split = len(parts) if step == 0 else -1
        ids = [device, jnp.transpose(item_owner, (0, 2, 1)), item_row, fifo_head[None]]
        ids = ids if small and step == 0 else []
        outs, extra = [(matrix, f32), (matrix, f32), (scalars, f32)], []
        if step == 0:
            extra = [places[None, :]]
            outs += [(matrix, bf16), (matrix, bf16), ((8 + queue_rows * bool(ids), query_count), f32), ((8, width), f32)]
            outs += [((queue_rows, width), f32)] if ids else []
        query_unit, found, sums, *rest = call(
            functools.partial(first_kernel, step, len(parts[:split]), len(ids)),
            outs,
            queries,
            found_at[None, :],
            negatives,
            *ids,
            *parts[:split],
            *extra,
        )
        if step == 0:
            away, half, notes, top, *own = rest
            told, unit = own[0] if ids else own_told(), found
            mine = [away, half, notes, told]
            beside = [flip(notes, masks[-1])]
            beside.append(beside[0][8:, :width] if ids else flip(told, masks[-1]))
            quarter = query_count // 2
            for part in (half, away):
                pieces = [part[i * quarter : (i + 1) * quarter] for i in range(2)]
                beside.insert(0, jnp.concatenate([flip(piece, masks[-1]) for piece in pieces]))
            if small:
                lines = [queue, queue]
            else:
                lines = [negatives.reshape(1, query_count)]
                lines.append(flip(lines[0], masks[-1]))
            outs = [((half_rows, width), f32)]
            (kept,) = call(functools.partial(start_kernel, stride, False), outs, *mine, lines[0])
            kernel = functools.partial(start_kernel, stride, True)
            (kept,) = call(kernel, outs, *beside, lines[1], kept)
            kept = grad_scale * kept
            for mask in masks[-2:0:-1]:
                middle = kept.shape[0] // 2
                kept, sent = kept[:middle], kept[middle:].astype(f16)
                kept = kept + flip(sent, mask).astype(f32)
            total, early = reduce_near(kept)
        else:
            sent, rows, unit, top = call(
                functools.partial(main_kernel, last_place, len(parts[split:]), stride),
                [((half_rows, width), bf16), (matrix, bf16), (matrix, f32), ((8, width), f32)],
                found,
                found_at[None, :],
                places[None, :],
                query_unit,
                sums,
                *parts[split:],
                told,
            )
            kernel = functools.partial(kept_kernel, stride)
            (kept,) = call(kernel, [((half_rows, width), f32)], places[None, :], rows, told)
            sent = (grad_scale * sent).astype(bf16)
            kept = grad_scale * kept
            for mask in masks[:1:-1]:
                kept = kept + flip(sent, mask).astype(f32)
                middle = kept.shape[0] // 2
                kept, sent = kept[:middle], kept[middle:].astype(f16)
            total, early = reduce_near(kept, flip(sent, masks[1]))
        tops.append(top)

        more = step + 1 < step_count
        args = [queries, unit, queue if small else negatives, early, *([] if small else [moment])]
        scalar = ((part_rows, 1), f32)
        half_shard = [((part_rows, width), f32), scalar, scalar]
        scale = score_scale / grad_scale
        if more:
            outs = [((1, query_count), f32), (matrix, bf16), (fifo.shape, bf16)]
            outs += half_shard + half_shard
            args += [fifo, jnp.full((1, 1), side), table, line]
        else:
            outs = [((step_count, query_count), f32), (queries.shape, bf16), (fifo.shape, bf16)]
            args += [loss, query_grad, fifo, fifo_head[None], *tops]
        kernel = functools.partial(late_kernel, step, not small, scale)
        loss, query_grad, fifo, *rest, zero = call(kernel, outs + [(total.shape, f32)], *args)
        mine, other = reduce_far(total, zero)
        if more:
            kernel, outs = functools.partial(update_kernel, scale), half_shard + half_shard[:1]
            *near, unit = call(kernel, outs, mine, *rest[:3])
            *far, far_unit = call(kernel, outs, other, *rest[3:])
            queue, zero = next_queue(queue, mine[part_rows:])
            parts = gather_whole(unit.astype(f16), far_unit.astype(f16))
        else:
            outs = [(table.shape, f32), (line.shape, f32)]
            args = [jnp.full((1, 1), side), mine, other, *near, *far]
            table, line = call(finish_kernel, outs, *args)

    return (loss, query_grad, table, line[0], fifo)


def solution(mesh):
    both = ("batch", "table")
    in_specs = (
        P(None, both, None),
        P(None, both, None),
        P(None, both),
        P("table", None),
        P("table"),
        P(both, None),
        P(both),
    )
    out_specs = (P(None, both), P(None, both, None), P("table", None), P("table"), P(both, None))
    return jax.shard_map(
        per_device, mesh=mesh, in_specs=in_specs, out_specs=out_specs, check_vma=False
    )
```

```python
import functools

import jax
import jax.numpy as jnp
from jax import lax
from jax.experimental import pallas as pl
from jax.experimental.pallas import tpu as pltpu
from jax.sharding import PartitionSpec as P

ENQ = 4
score_scale = 10.0
learn_rate = 0.3
epsilon = 1e-06
f32 = jnp.float32
bf16 = jnp.bfloat16
f16 = jnp.float16
VMEM = 10 * 2**20


def masks_of(count):
    masks = []
    while count > 1:
        assert count % 2 == 0
        count //= 2
        masks.append(count)
    return masks


def stages_of(count, stride):
    stages, count = [], count // stride
    while count > 1:
        radix = next(r for r in range(2, count + 1) if count % r == 0)
        stages.append((stride, radix))
        stride, count = stride * radix, count // radix
    return stages


def flip(piece, mask):
    count = lax.axis_size("batch") * lax.axis_size("table")
    return lax.ppermute(piece, ("batch", "table"), [(i ^ mask, i) for i in range(count)])


def turned(piece, stride, radix):
    count = lax.axis_size("batch")
    found = []
    for turn in range(1, radix):
        pairs = []
        for target in range(count):
            digit = target // stride % radix
            pairs.append((target + ((digit + turn) % radix - digit) * stride, target))
        found.append(lax.ppermute(piece, "batch", pairs))
    return found


def sum_stage(total, stride, radix, zero=0.0):
    sent = lax.optimization_barrier(total.astype(f16))
    parts = jnp.stack([sent] + turned(sent, stride, radix)) if radix > 2 else None
    if radix > 2:
        digit = lax.axis_index("batch") // stride % radix
        parts = list(parts[(jnp.arange(radix, dtype=jnp.int32) - digit) % radix])
    else:
        parts = [sent] + turned(sent, stride, radix)
    total = parts[0].astype(f32) + zero
    for part in parts[1:]:
        total = total + part.astype(f32)
    return total


def split_parts(rows, terms):
    parts = []
    for _ in range(terms):
        part = lax.reduce_precision(rows, 8, 7)
        parts.append(part.astype(bf16))
        rows = rows - part
    return jnp.concatenate(parts, 1)


def pick_rows(places, blocks, width):
    total, first = None, 0
    for block in blocks:
        count = block.shape[0]
        chosen = (places[:, None] - first == jnp.arange(count, dtype=jnp.int32)[None, :]).astype(bf16)
        found = jnp.dot(chosen, block, preferred_element_type=f32)
        rows = found[:, :width]
        for start in range(width, block.shape[1], width):
            rows = rows + found[:, start : start + width]
        total = rows if total is None else total + rows
        first += count
    return total


def score_piece(query_half, carried, rows, kept):
    total_sum, moment = carried
    scores = score_scale * lax.dot_general(
        query_half, rows, (((1,), (1,)), ((), ())), preferred_element_type=f32
    )
    weights = jnp.where(kept[None, :], jnp.exp(scores), 0.0)
    moment = moment + jnp.dot(weights.astype(bf16), rows, preferred_element_type=f32)
    return (total_sum + jnp.sum(weights, 1), moment)


def score_rows(query_half, rows, kept):
    count, width = rows.shape
    carried = (jnp.zeros(query_half.shape[:1], f32), jnp.zeros(query_half.shape, f32))
    splits = 1
    while count // splits > 1024 and count % (splits * 2) == 0:
        splits = splits * 2
    if splits == 1:
        return score_piece(query_half, carried, rows, kept)
    stacked = (rows.reshape(splits, -1, width), kept.reshape(splits, -1))
    return lax.scan(lambda c, b: (score_piece(query_half, c, *b), None), carried, stacked)[0]


def norm_of(rows):
    return jnp.sqrt(jnp.sum(rows * rows, 1) + epsilon)


def one_hot(places, first, count, columns):
    shape = (places.shape[0], count) if columns else (count, places.shape[1])
    numbers = lax.broadcasted_iota(jnp.int32, shape, 1 if columns else 0)
    return (numbers == places - first).astype(f32).astype(bf16)


def column(line):
    count = line.shape[1]
    tall = jnp.broadcast_to(line, (128, count))
    return jnp.transpose(jnp.pad(tall, ((0, 0), (0, -count % 128))))[:count, :1]


def split_dot(places, blocks, first=0):
    found = 0.0
    for block in blocks:
        count, width = block.shape
        chosen = one_hot(places, first, count, True)
        first += count
        rows = block[...]
        high = rows.astype(bf16)
        low = (rows - high.astype(f32)).astype(bf16)
        both = jnp.concatenate([high, low], 1)
        found = found + jnp.dot(chosen, both, preferred_element_type=f32)
    return found[:, :width] + found[:, width:]


def unit_of(rows):
    norm = jnp.sqrt(jnp.sum(rows * rows, 1, keepdims=True) + epsilon)
    return rows / norm, norm


def weights_of(unit, negatives):
    scores = lax.dot_general(
        unit.astype(bf16), negatives, (((1,), (1,)), ((), ())), preferred_element_type=f32
    )
    return jnp.exp(score_scale * scores)


def told_block(device, owner, row, head, queue_rows, width):
    line = lax.broadcasted_iota(jnp.int32, (queue_rows, width), 0)
    lane = lax.broadcasted_iota(jnp.int32, (queue_rows, width), 1)
    part = jnp.where(lane // 4 == device[...], lane % 4, -1)
    told = jnp.zeros((queue_rows, width), jnp.int32)
    for k in range(ENQ):
        item, number = owner[0, :, k : k + 1], row[0:1, k : k + 1]
        values = jnp.where(part == 0, item + 1, jnp.where(part == 1, number // 16, number % 16))
        values = jnp.where((part >= 0) & (part < 3), values, 0)
        told = jnp.where(line == lax.rem(head[...] + k, queue_rows), values, told)
    return told.astype(f32)


def first_kernel(step, count, scalars, queries, line, negatives, *refs):
    ids, blocks, refs = refs[:scalars], refs[scalars : scalars + count], refs[scalars + count :]
    if step == 0:
        places, unit, found, sums, *told = refs
        told = (places, *told)
    else:
        unit, found, sums = refs
    unit[...], _ = unit_of(queries[step].astype(f32))
    item = split_dot(column(line[...]), blocks)
    found[...] = unit_of(item)[0] if step == 0 else item
    if negatives.shape[1] > 1:
        sums[...] = jnp.sum(weights_of(unit[...], negatives[...]), 1, keepdims=True)
    else:
        sums[...] = negatives[...]
    if step == 0:
        places, away, half, notes, top, *told = told
        query, item = unit[...], found[...]
        cosine = jnp.sum(query * item, 1, keepdims=True)
        away[...] = (query - item * cosine).astype(bf16)
        half[...] = query.astype(bf16)
        spread = jnp.broadcast_to(score_scale * cosine, item.shape)
        weight = jnp.exp(jnp.transpose(spread)[:1])
        line = places[...].astype(f32)
        notes[:8, :] = jnp.concatenate([weight, line, jnp.zeros((6, line.shape[1]), f32)])
        top[...] = item[: top.shape[0]]
        if told:
            block = told_block(*ids, *told[0].shape)
            told[0][...] = block
            gap = jnp.zeros((block.shape[0], line.shape[1] - block.shape[1]), f32)
            notes[8:, :] = jnp.concatenate([block, gap], 1)


def main_kernel(first, count, stride, found, found_line, line, queries, negatives, *refs):
    blocks, (told, sent, rows, unit, top) = refs[:count], refs[count:]
    item = found[...]
    if blocks:
        item = item + split_dot(column(found_line[...]), blocks, first)
    unit[...] = item
    top[...] = item[: top.shape[0]]
    query = queries[...]
    if negatives.shape[1] > 1:
        sums = jnp.sum(weights_of(query, negatives[...]), 1, keepdims=True)
    else:
        sums = negatives[...]
    cosine = jnp.sum(query * item, 1, keepdims=True)
    weight = jnp.exp(score_scale * cosine)
    lack = weight / (weight + sums) - 1.0
    rows[...] = (lack * (query - item * cosine)).astype(bf16)
    dense(sent.shape[0], stride, line, rows, told, sent)


def dense_rows(first, half, stride, line, rows, told, lack=1.0):
    count = told.shape[0]
    numbers = lax.broadcasted_iota(jnp.int32, (half, rows.shape[0]), 0)
    chosen = jnp.where(numbers == line - first, lack, 0.0).astype(bf16)
    found = jnp.dot(chosen, rows, preferred_element_type=f32)
    pieces = []
    for start in range(0, half, stride):
        pieces += [found[start : start + stride - count], told]
    return jnp.concatenate(pieces)


def dense(first, stride, line, rows, told, out):
    found = dense_rows(first, out.shape[0], stride, line[...], rows[...], told[...])
    out[...] = found.astype(out.dtype)


def start_kernel(stride, far, away, half, notes, told, negatives, *refs):
    out = refs[-1]
    if negatives.dtype == bf16:
        scores = lax.dot_general(
            negatives[...], half[...], (((1,), (1,)), ((), ())), preferred_element_type=f32
        )
        sums = jnp.sum(jnp.exp(score_scale * scores), 0, keepdims=True)
    else:
        sums = negatives[...]
    weight, line = notes[0:1, :], notes[1:2, :].astype(jnp.int32)
    lack = weight / (weight + sums) - 1.0
    count = out.shape[0]
    rows = dense_rows(count if far else 0, count, stride, line, away[...], told[...], lack)
    out[...] = rows + refs[0][...] if far else rows


def kept_kernel(stride, line, rows, told, out):
    dense(0, stride, line, rows, told, out)


def late_kernel(step, given, scale, queries, item, negatives, _, *refs):
    query, query_norm = unit_of(queries[step].astype(f32))
    if given:
        moment, sums, refs = refs[0][...], negatives[...], refs[1:]
    else:
        weights = weights_of(query, negatives[...])
        sums = jnp.sum(weights, 1, keepdims=True)
        moment = jnp.dot(weights.astype(bf16), negatives[...], preferred_element_type=f32)
    item = item[...]
    score = score_scale * jnp.sum(query * item, 1, keepdims=True)
    weight = jnp.exp(score)
    total = weight + sums
    loss = jnp.transpose(jnp.broadcast_to(jnp.log(total) - score, item.shape))[:1]
    unit_grad = score_scale * ((weight / total - 1.0) * item + moment / total)
    along = jnp.sum(query * unit_grad, 1, keepdims=True)
    grad = ((unit_grad - query * along) / query_norm).astype(bf16)
    zero, refs = refs[-1], refs[:-1]
    zero[...] = jnp.zeros_like(zero)
    if step == 0:
        fifo, side, table, accum, loss_out, grad_out, fifo_out, *halves = refs
        loss_out[...], grad_out[...], fifo_out[...] = loss, grad, fifo[...]
        rows = table[...]
        values = (rows, column(accum[...]), scale / unit_of(rows)[1])
        first, count = side[...] == 0, halves[0].shape[0]
        for near, far, value in zip(halves[:3], halves[3:], values):
            low, high = value[:count], value[count:]
            near[...], far[...] = jnp.where(first, low, high), jnp.where(first, high, low)
        return
    loss_before, grad_before, fifo, head, *tops, losses, grads, fifo_out = refs
    losses[0:1, :], losses[1:2, :] = loss_before[...], loss
    grads[0], grads[1] = grad_before[...], grad
    queue_rows = fifo.shape[0]
    line = lax.broadcasted_iota(jnp.int32, fifo.shape, 0)
    queue = fifo[...].astype(f32)
    for number, top in enumerate(tops):
        for k in range(ENQ):
            slot = lax.rem(head[...] + (number * ENQ + k), queue_rows)
            queue = jnp.where(line == slot, top[k : k + 1, :], queue)
    fifo_out[...] = queue.astype(bf16)


def queue_kernel(count, told, negatives, *refs):
    blocks, (out, zero) = refs[:count], refs[count:]
    item, _ = unit_of(split_dot(told[...], blocks))
    zero[...] = jnp.zeros_like(zero)
    out[...] = jnp.where(told[...] >= 0, item, negatives[...].astype(f32)).astype(bf16)


def adagrad(grad, table, accum, inverse):
    grad = grad * inverse
    accum = accum + jnp.mean(grad * grad, 1, keepdims=True)
    return table - learn_rate * grad / jnp.sqrt(accum), accum


def update_kernel(scale, total, table, accum, inverse, table_out, accum_out, *more):
    grad = total[: table.shape[0], :]
    rows, accum_out[...] = adagrad(grad, table[...], accum[...], inverse[...])
    table_out[...] = rows
    if more:
        inverse_out, unit = more
        unit[...], norm = unit_of(rows)
        inverse_out[...] = scale / norm


def finish_kernel(side, other, near_table, near_accum, table, accum, inverse, table_out, line_out):
    count, first = table.shape[0], side[...] == 0
    rows, far = adagrad(other[:count, :], table[...], accum[...], inverse[...])
    near_rows, near = near_table[...], near_accum[...]
    table_out[:count, :] = jnp.where(first, near_rows, rows)
    table_out[count:, :] = jnp.where(first, rows, near_rows)
    tall = jnp.concatenate([jnp.where(first, near, far), jnp.where(first, far, near)])
    wide = jnp.pad(tall, ((0, -2 * count % 128), (0, 0)))
    wide = jnp.broadcast_to(wide, (wide.shape[0], 128))
    line_out[...] = jnp.transpose(wide)[:1, : 2 * count]


def call(kernel, outs, *args):
    vmem = pl.BlockSpec(memory_space=pltpu.VMEM)
    return pl.pallas_call(
        kernel,
        out_shape=[jax.ShapeDtypeStruct(shape, dtype) for shape, dtype in outs],
        in_specs=[vmem] * len(args),
        out_specs=[vmem] * len(outs),
        compiler_params=pltpu.CompilerParams(vmem_limit_bytes=VMEM),
    )(*args)


def per_device(queries, item_owner, item_row, table, accum, fifo, fifo_head):
    step_count, query_count, width = queries.shape
    owners, copies = lax.axis_size("table"), lax.axis_size("batch")
    owned = table.shape[0]
    part_rows = owned // 2
    queue_rows = fifo.shape[0]
    devices = owners * copies
    lanes = width // 4
    tiles = -(-devices // lanes)
    stride = part_rows + tiles * queue_rows
    half_rows = owners * stride
    me = lax.axis_index("table")
    side = lax.axis_index("batch") % 2
    masks = masks_of(owners)
    small = devices * queue_rows <= 1024 and tiles == 1
    most = owners * copies * (3 * query_count // owners)
    grad_scale = 1.0
    while most * grad_scale > 32768.0:
        grad_scale = grad_scale / 2

    def owner_place(owner):
        apart = jnp.bitwise_xor(owner, me)
        place = jnp.zeros_like(owner)
        for index, mask in enumerate(masks):
            place = place + jnp.where((apart & mask) != 0, 1 << index, 0)
        return place

    def place_whole(owner, row):
        return owner_place(owner) * owned + row

    def place_part(owner, row, stride):
        half = row // part_rows
        return (2 * owner_place(owner) + jnp.bitwise_xor(half, side)) * stride + row % part_rows

    def gather_whole(*pieces):
        pieces = list(pieces)
        for mask in masks:
            pieces = pieces + [flip(piece, mask) for piece in pieces]
        return pieces

    def reduce_near(kept, came=None):
        spans = [slice(i * stride, (i + 1) * stride) for i in range(4)]
        pieces = [kept[span] for span in spans]
        if came is not None:
            pieces = [piece + came[span].astype(f32) for piece, span in zip(pieces, spans)]
        near = [
            flip(piece.astype(f16), mask)
            for piece, mask in zip(pieces[1:], (owners, masks[0], owners + masks[0]))
        ]
        beside = [piece.astype(f32) for piece in near]
        return (pieces[0] + beside[0]) + (beside[1] + beside[2]), near[0][:8].astype(f32)

    def reduce_far(total, zero):
        stages = stages_of(copies, 2)
        paired = stages[:1] == [(2, 2)]
        for stage in stages[paired:]:
            total = sum_stage(total, *stage, zero)
        sent = lax.optimization_barrier(total.astype(f16))
        if paired:
            pairs = [[sent, flip(sent, 2 * owners)], [flip(sent, owners), flip(sent, 3 * owners)]]
        else:
            pairs = [[sent], [flip(sent, owners)]]
        return [sum(part.astype(f32) for part in pair) for pair in pairs]

    def own_told():
        slot = jnp.arange(queue_rows, dtype=jnp.int32)[:, None]
        taken = (slot - fifo_head) % queue_rows == jnp.arange(ENQ, dtype=jnp.int32)
        owner, row = item_owner[0, :ENQ, 0], item_row[0, :ENQ]
        told = [jnp.sum(jnp.where(taken, part, 0), 1) for part in (owner + 1, row // 16, row % 16)]
        told = jnp.stack(told + [jnp.zeros((queue_rows,), jnp.int32)], 1).astype(f32)
        mine = jnp.arange(tiles * lanes, dtype=jnp.int32) == lax.axis_index(("batch", "table"))
        told = jnp.where(mine[:, None, None], told, 0.0).reshape(tiles, lanes, queue_rows, 4)
        return told.transpose(0, 2, 1, 3).reshape(tiles * queue_rows, width)

    def next_queue(queue, told):
        told = (told / grad_scale).reshape(tiles, queue_rows, lanes, 4).transpose(0, 2, 1, 3)
        told = told.reshape(-1, 4)[: devices * queue_rows].astype(jnp.int32)
        place = place_whole(told[:, 0] - 1, told[:, 1] * 16 + told[:, 2])
        place = jnp.where(told[:, 0] > 0, place, -1)[:, None]
        if small:
            kernel = functools.partial(queue_kernel, len(parts))
            queue, zero = call(kernel, [(queue.shape, bf16), ((part_rows, width), f32)], place, queue, *parts)
            return queue, zero
        blocks = [split_parts(part, 2) for part in parts]
        new = lax.map(lambda at: pick_rows(at, blocks, width), place.reshape(-1, copies * queue_rows))
        return jnp.where(place >= 0, unit_of(new.reshape(queue.shape))[0].astype(bf16), queue), 0.0

    parts = gather_whole(table)

    queue = jnp.broadcast_to(jnp.maximum(fifo, bf16(-3e38))[None], (devices, *fifo.shape))
    queue = lax.all_to_all(queue, ("batch", "table"), 0, 0, tiled=True).reshape(-1, width)
    device = jnp.full((1, 1), lax.axis_index(("batch", "table")))

    line = accum[None, :]
    tops = []
    for step in range(step_count):
        owner, row = item_owner[step, :, 0], item_row[step]
        places = place_part(owner, row, stride)
        found_at = place_part(owner, row, part_rows) if step else place_whole(owner, row)
        last_place = owners * owned - parts[-1].shape[0]
        parts = [part.astype(f32) for part in parts]
        if step:
            parts[3] = parts[3] + zero
        scalars, matrix = (query_count, 1), (query_count, width)
        if small:
            negatives = queue if step else jnp.zeros(scalars, f32)
        else:
            query_half = unit_of(queries[step].astype(f32))[0].astype(bf16)
            negatives, moment = score_rows(query_half, queue, jnp.ones(queue.shape[:1], jnp.bool_))
            negatives = negatives[:, None]
        split = len(parts) if step == 0 else -1
        ids = [device, jnp.transpose(item_owner, (0, 2, 1)), item_row, fifo_head[None]]
        ids = ids if small and step == 0 else []
        outs, extra = [(matrix, f32), (matrix, f32), (scalars, f32)], []
        if step == 0:
            extra = [places[None, :]]
            outs += [(matrix, bf16), (matrix, bf16), ((8 + queue_rows * bool(ids), query_count), f32), ((8, width), f32)]
            outs += [((queue_rows, width), f32)] if ids else []
        query_unit, found, sums, *rest = call(
            functools.partial(first_kernel, step, len(parts[:split]), len(ids)),
            outs,
            queries,
            found_at[None, :],
            negatives,
            *ids,
            *parts[:split],
            *extra,
        )
        if step == 0:
            away, half, notes, top, *own = rest
            told, unit = own[0] if ids else own_told(), found
            mine = [away, half, notes, told]
            beside = [flip(notes, masks[-1])]
            beside.append(beside[0][8:, :width] if ids else flip(told, masks[-1]))
            quarter = query_count // 2
            for part in (half, away):
                pieces = [part[i * quarter : (i + 1) * quarter] for i in range(2)]
                beside.insert(0, jnp.concatenate([flip(piece, masks[-1]) for piece in pieces]))
            if small:
                lines = [queue, queue]
            else:
                lines = [negatives.reshape(1, query_count)]
                lines.append(flip(lines[0], masks[-1]))
            outs = [((half_rows, width), f32)]
            (kept,) = call(functools.partial(start_kernel, stride, False), outs, *mine, lines[0])
            kernel = functools.partial(start_kernel, stride, True)
            (kept,) = call(kernel, outs, *beside, lines[1], kept)
            kept = grad_scale * kept
            for mask in masks[-2:0:-1]:
                middle = kept.shape[0] // 2
                kept, sent = kept[:middle], kept[middle:].astype(f16)
                kept = kept + flip(sent, mask).astype(f32)
            total, early = reduce_near(kept)
        else:
            sent, rows, unit, top = call(
                functools.partial(main_kernel, last_place, len(parts[split:]), stride),
                [((half_rows, width), bf16), (matrix, bf16), (matrix, f32), ((8, width), f32)],
                found,
                found_at[None, :],
                places[None, :],
                query_unit,
                sums,
                *parts[split:],
                told,
            )
            kernel = functools.partial(kept_kernel, stride)
            (kept,) = call(kernel, [((half_rows, width), f32)], places[None, :], rows, told)
            sent = (grad_scale * sent).astype(bf16)
            kept = grad_scale * kept
            for mask in masks[:1:-1]:
                kept = kept + flip(sent, mask).astype(f32)
                middle = kept.shape[0] // 2
                kept, sent = kept[:middle], kept[middle:].astype(f16)
            total, early = reduce_near(kept, flip(sent, masks[1]))
        tops.append(top)

        more = step + 1 < step_count
        args = [queries, unit, queue if small else negatives, early, *([] if small else [moment])]
        scalar = ((part_rows, 1), f32)
        half_shard = [((part_rows, width), f32), scalar, scalar]
        scale = score_scale / grad_scale
        if more:
            outs = [((1, query_count), f32), (matrix, bf16), (fifo.shape, bf16)]
            outs += half_shard + half_shard
            args += [fifo, jnp.full((1, 1), side), table, line]
        else:
            outs = [((step_count, query_count), f32), (queries.shape, bf16), (fifo.shape, bf16)]
            args += [loss, query_grad, fifo, fifo_head[None], *tops]
        kernel = functools.partial(late_kernel, step, not small, scale)
        loss, query_grad, fifo, *rest, zero = call(kernel, outs + [(total.shape, f32)], *args)
        mine, other = reduce_far(total, zero)
        if more:
            kernel, outs = functools.partial(update_kernel, scale), half_shard + half_shard[:1]
            *near, unit = call(kernel, outs, mine, *rest[:3])
            *far, far_unit = call(kernel, outs, other, *rest[3:])
            queue, zero = next_queue(queue, mine[part_rows:])
            parts = gather_whole(unit.astype(f16), far_unit.astype(f16))
        else:
            outs = [(table.shape, f32), (line.shape, f32)]
            kernel = functools.partial(update_kernel, scale)
            near = call(kernel, half_shard[:2], mine, *near)
            args = [jnp.full((1, 1), side), other, *near, *far]
            table, line = call(finish_kernel, outs, *args)

    return (loss, query_grad, table, line[0], fifo)


def solution(mesh):
    both = ("batch", "table")
    in_specs = (
        P(None, both, None),
        P(None, both, None),
        P(None, both),
        P("table", None),
        P("table"),
        P(both, None),
        P(both),
    )
    out_specs = (P(None, both), P(None, both, None), P("table", None), P("table"), P(both, None))
    return jax.shard_map(
        per_device, mesh=mesh, in_specs=in_specs, out_specs=out_specs, check_vma=False
    )
```
